128 devices in a mesh: dp: 16 (over x_hi, z, core), space: 8 (over x_lo, y).
Axes of the slice: x: 4 (x_hi: 2, x_lo: 2; x = x_hi * 2 + x_lo), y: 4, z: 4, core: 2. Of those that a mesh axis runs over, the one named last changes fastest.
Arguments:
- query: bfloat16 [16, 3072, 1536], P('dp', 'space'), may hold values from -8 to 8
- key_in: bfloat16 [16, 3072, 1536], P('dp', 'space'), may hold values from -8 to 8
- value_in: bfloat16 [16, 3072, 1536], P('dp', 'space'), may hold values from -6 to 6
- out_weight: bfloat16 [1536, 3072], P('dp'), may hold values from -0.15625 to 0.15625
- grad_out: bfloat16 [16, 3072, 3072], P('dp', 'space'), may hold values from -6 to 6
- neighbours: int32 [8, 3], replicated, may hold values from -1 to 7, as said below
Outputs:
- mixed: bfloat16 [16, 3072, 3072], P('dp', 'space')
- grad_query: bfloat16 [16, 3072, 1536], P('dp', 'space')
- grad_key: bfloat16 [16, 3072, 1536], P('dp', 'space')
- grad_value: bfloat16 [16, 3072, 1536], P('dp', 'space')
- grad_weight: float32 [1536, 3072], P('dp')
The draws below stay inside these ranges and needn't reach their ends.
Inputs may be any that keep to these rules, and one draw needn't show every extreme that they name: `neighbours`: entry 0 of row t is t; entry 1 is t - 1 or -1; entry 2 is t + 1 or -1.
All inputs are finite; a program needn't handle non-finite values.
Results may differ from the reference program's by a relative error of at most 0.034.
Values may be sent and summed in bfloat16 or wider, within the bound.
No kernel may reach another device: no remote copies, remote signals or barrier semaphores. Data moves between devices by JAX's collectives and lax.ppermute only.
A program may use at most 192 MiB of HBM per device.

```python
import math
import jax
import jax.numpy as jnp
from jax import lax

D = 3072
HEADS = 12
HEAD = 128
TILE = 384
HD = 1536
TILES = 8
TOKENS = 3072
CLIPS = 16


def draw_query(key, part):
    key = jax.random.fold_in(key, 101)
    values = jnp.clip(jax.random.normal(key, (CLIPS, TOKENS, HD), jnp.float32), -6.0, 6.0)
    return values.astype(jnp.bfloat16)


def draw_key_in(key, part):
    key = jax.random.fold_in(key, 202)
    values = jnp.clip(jax.random.normal(key, (CLIPS, TOKENS, HD), jnp.float32), -6.0, 6.0)
    return values.astype(jnp.bfloat16)


def draw_neighbours(key, part):
    key = jax.random.fold_in(key, 303)
    tile_ids = jnp.arange(TILES, dtype=jnp.int32)
    living = jax.random.randint(key, (TILES, 2), 0, 3) > 0
    left_ids = jnp.where(living[:, 0] & (tile_ids >= 1), tile_ids - 1, -1)
    right_ids = jnp.where(living[:, 1] & (tile_ids < TILES - 1), tile_ids + 1, -1)
    return jnp.stack([tile_ids, left_ids, right_ids], axis=1).astype(jnp.int32)


def block_levels(own_key, extent, pieces, smallest, largest):
    level = 1.0
    for dim, shards_of in pieces:
        steps = jax.random.uniform(jax.random.fold_in(jax.random.fold_in(own_key, 6), dim), (shards_of,), jnp.float32, smallest / len(pieces), largest / len(pieces))
        level = level * jnp.repeat(jnp.exp(steps), extent[dim] // shards_of).reshape((-1,) + (1,) * (len(extent) - 1 - dim))
    return level


def normal_values(rng, dims, deviation, bound, shards=(), held_as=jnp.bfloat16):
    gain = block_levels(rng, dims, shards, -0.22, 0.18) if shards else 1.0
    array = jax.random.normal(rng, dims, jnp.float32) * deviation * gain
    return jnp.minimum(jnp.maximum(array, -bound), bound).astype(held_as)


def setup_inputs(seed: int = 0) -> dict:
    key_of = jax.random.split(jax.random.key(seed), 7)
    query = draw_query(jax.random.fold_in(key_of[6], 71), 0)
    key_in = draw_key_in(jax.random.fold_in(key_of[6], 71), 0)
    value_in = normal_values(key_of[2], (CLIPS, TOKENS, HD), 1.0, 6.0, ((0, 16), (1, 8)))
    out_weight = normal_values(key_of[3], (HD, D), HD ** -0.5, 0.15625, ((0, 16),))
    grad_out = normal_values(key_of[4], (CLIPS, TOKENS, D), 1.0, 6.0, ((0, 16), (1, 8)))
    neighbours = draw_neighbours(jax.random.fold_in(key_of[6], 71), 0)
    return dict(query=query, key_in=key_in, value_in=value_in, out_weight=out_weight, grad_out=grad_out, neighbours=neighbours)


masked_score = -1e+30

def tile_window(blocks, axis):
    padding = [(1, 1)] + [(0, 0)] * (blocks.ndim - 1)
    padded = jnp.pad(blocks, padding)
    return jnp.concatenate([padded[:-2], padded[1:-1], padded[2:]], axis=axis)

def rounded(values):
    return lax.optimization_barrier(values.astype(jnp.bfloat16))

def reference(query, key_in, value_in, out_weight, grad_out, neighbours):
    tile_total = TOKENS // TILE
    score_scale = 1.0 / math.sqrt(HEAD)
    tile_ids = jnp.arange(tile_total, dtype=jnp.int32)
    window_tiles = tile_ids[:, None] - 1 + jnp.arange(3, dtype=jnp.int32)[None, :]
    key_live = jnp.any((neighbours[:, None, :] == window_tiles[:, :, None]) & (neighbours[:, None, :] >= 0), axis=2)
    inside = (window_tiles >= 0) & (window_tiles < tile_total)
    their_lists = neighbours[jnp.clip(window_tiles, 0, tile_total - 1)]
    query_live = inside & jnp.any(their_lists == tile_ids[:, None, None], axis=2)
    key_mask = jnp.repeat(key_live, TILE, axis=1)
    query_mask = jnp.repeat(query_live, TILE, axis=1)
    shape_four = (tile_total, TILE, HEADS, HEAD)
    shape_wide = (tile_total, 3 * TILE, HEADS, HEAD)

    def one_clip(inputs):
        query_rows, key_rows, value_rows, upstream = inputs
        queries = query_rows.reshape(shape_four).astype(jnp.float32)
        keys_own = key_rows.reshape(shape_four).astype(jnp.float32)
        values_own = value_rows.reshape(shape_four).astype(jnp.float32)
        key_window = tile_window(key_rows.reshape(tile_total, TILE, HD), 1).reshape(shape_wide).astype(jnp.float32)
        value_window = tile_window(value_rows.reshape(tile_total, TILE, HD), 1).reshape(shape_wide).astype(jnp.float32)
        scores = jnp.einsum('tihd,tjhd->thij', queries, key_window) * score_scale
        scores = jnp.where(key_mask[:, None, None, :], scores, masked_score)
        row_max = lax.optimization_barrier(jnp.max(scores, axis=3, keepdims=True))
        log_total = (row_max + jnp.log(lax.optimization_barrier(jnp.sum(jnp.exp(scores - row_max), axis=3, keepdims=True))))[..., 0]
        weights = jnp.exp(scores - log_total[..., None])
        weights_bf = rounded(weights).astype(jnp.float32)
        attn = rounded(jnp.einsum('thij,tjhd->tihd', weights_bf, value_window).reshape(TOKENS, HD))
        mixed = jnp.dot(attn, out_weight, preferred_element_type=jnp.float32).astype(jnp.bfloat16)
        grad_attn = rounded(lax.dot_general(upstream, out_weight, (((1,), (1,)), ((), ())), preferred_element_type=jnp.float32))
        grad_heads = grad_attn.reshape(shape_four).astype(jnp.float32)
        deltas = lax.optimization_barrier(jnp.sum(grad_heads * attn.reshape(shape_four).astype(jnp.float32), axis=3)).transpose(0, 2, 1)
        dprob = jnp.einsum('tihd,tjhd->thij', grad_heads, value_window)
        dscore = rounded(weights * (dprob - deltas[..., None]) * score_scale).astype(jnp.float32)
        grad_query = jnp.einsum('thij,tjhd->tihd', dscore, key_window).reshape(TOKENS, HD).astype(jnp.bfloat16)
        query_window = tile_window(query_rows.reshape(tile_total, TILE, HD), 1).reshape(shape_wide).astype(jnp.float32)
        grad_window = tile_window(grad_attn.reshape(tile_total, TILE, HD), 1).reshape(shape_wide).astype(jnp.float32)
        log_window = tile_window(log_total, 2)
        delta_window = tile_window(deltas, 2)
        back_scores = jnp.einsum('tjhd,tihd->thji', query_window, keys_own) * score_scale
        back_weights = jnp.where(query_mask[:, None, :, None], jnp.exp(back_scores - log_window[..., None]), 0.0)
        back_bf = rounded(back_weights).astype(jnp.float32)
        grad_value = jnp.einsum('thji,tjhd->tihd', back_bf, grad_window).reshape(TOKENS, HD).astype(jnp.bfloat16)
        back_dprob = jnp.einsum('tjhd,tihd->thji', grad_window, values_own)
        back_dscore = rounded(back_weights * (back_dprob - delta_window[..., None]) * score_scale).astype(jnp.float32)
        grad_key = jnp.einsum('thji,tjhd->tihd', back_dscore, query_window).reshape(TOKENS, HD).astype(jnp.bfloat16)
        return (mixed, grad_query, grad_key, grad_value, attn)
    mixed, grad_query, grad_key, grad_value, attn_all = lax.map(one_clip, (query, key_in, value_in, grad_out))
    grad_weight = lax.dot_general(attn_all.reshape(CLIPS * TOKENS, HD), grad_out.reshape(CLIPS * TOKENS, D), (((0,), (0,)), ((), ())), preferred_element_type=jnp.float32)
    return (mixed, grad_query, grad_key, grad_value, grad_weight)
```

```python
import functools
import math

import jax
import jax.numpy as jnp
from jax import lax
from jax.experimental import pallas as pl
from jax.experimental.pallas import tpu as pltpu
from jax.sharding import PartitionSpec as P

HEAD = 128
SCALE = 1.0 / math.sqrt(HEAD)
LOG2_SCALE = SCALE * math.log2(math.e)
FAR = 1e30
BF = jnp.bfloat16
F32 = jnp.float32
VMEM_LIMIT = 56 * 1024 * 1024

NX, NZ, NC, NL, NY = 2, 4, 2, 2, 4
NS = NL * NY


def moves(change):
    pairs = []
    for a in range(NX):
        for z in range(NZ):
            for c in range(NC):
                for l in range(NL):
                    for y in range(NY):
                        b, w, d, m, v = change(a, z, c, l, y)
                        src = ((a * NZ + z) * NC + c) * NS + l * NY + y
                        dst = ((b * NZ + w) * NC + d) * NS + m * NY + v
                        pairs.append((src, dst))
    return pairs


def move(x, change):
    return lax.ppermute(x, ("dp", "space"), moves(change))


def move_core(x):
    return move(x, lambda a, z, c, l, y: (a, z, 1 - c, l, y))


def move_lo(x):
    return move(x, lambda a, z, c, l, y: (a, z, c, 1 - l, y))


def move_lo_core(x):
    return move(x, lambda a, z, c, l, y: (a, z, 1 - c, 1 - l, y))


def move_hi(x):
    return move(x, lambda a, z, c, l, y: (1 - a, z, c, l, y))


def move_cross(x):
    return move(x, lambda a, z, c, l, y: (1 - a, z, c, 1 - l, y))


def move_z(x, k):
    return move(x, lambda a, z, c, l, y: (a, (z + k) % NZ, c, l, y))


def move_y(x, k):
    return move(x, lambda a, z, c, l, y: (a, z, c, l, (y + k) % NY))


def to_next(x):
    return lax.ppermute(x, "space", [(i, i + 1) for i in range(NS - 1)])


def to_previous(x):
    return lax.ppermute(x, "space", [(i + 1, i) for i in range(NS - 1)])


def nt(a, b):
    return lax.dot_general(a, b, (((1,), (1,)), ((), ())), preferred_element_type=F32)


def tn(a, b):
    return lax.dot_general(a, b, (((0,), (0,)), ((), ())), preferred_element_type=F32)


def nn(a, b):
    return lax.dot_general(a, b, (((1,), (0,)), ((), ())), preferred_element_type=F32)


def forward_kernel(info, q_ref, k_ref, v_ref, left_ref, right_ref, attn_ref, total_ref):
    q = q_ref[...]
    tiles = ((left_ref[0], left_ref[1]), (k_ref[...], v_ref[...]), (right_ref[0], right_ref[1]))
    live = (info[1] > 0, None, info[2] > 0)
    scores = [nt(k, q) for k, _ in tiles]
    tops = [jnp.max(s, axis=0, keepdims=True) for s in scores]
    top = tops[1]
    for j in (0, 2):
        top = jnp.maximum(top, jnp.where(live[j], tops[j], -FAR))
    top = top * LOG2_SCALE
    total = jnp.zeros_like(top)
    acc = jnp.zeros((HEAD, q.shape[0]), F32)
    for j in range(3):
        if live[j] is None:
            factor, shift = LOG2_SCALE, top
        else:
            factor = jnp.where(live[j], LOG2_SCALE, 0.0)
            shift = jnp.where(live[j], top, FAR)
        p = jnp.exp2(scores[j] * factor - shift)
        total = total + jnp.sum(p, axis=0, keepdims=True)
        acc = acc + tn(tiles[j][1], p.astype(BF))
    attn_ref[...] = (acc / total).astype(BF)
    total_ref[0] = top + jnp.log2(total)


def attend(info, q, k, v, left, right, heads):
    rows = q.shape[0]
    own = pl.BlockSpec((rows, HEAD), lambda h, info: (0, info[0] + h))
    side = pl.BlockSpec((2, rows, HEAD), lambda h, info: (0, 0, h))
    return pl.pallas_call(
        forward_kernel,
        out_shape=(
            jax.ShapeDtypeStruct((heads * HEAD, rows), BF),
            jax.ShapeDtypeStruct((heads, 1, rows), F32),
        ),
        grid_spec=pltpu.PrefetchScalarGridSpec(
            num_scalar_prefetch=1,
            grid=(heads,),
            in_specs=[own, own, own, side, side],
            out_specs=(
                pl.BlockSpec((HEAD, rows), lambda h, info: (h, 0)),
                pl.BlockSpec((1, 1, rows), lambda h, info: (h, 0, 0)),
            ),
        ),
        compiler_params=pltpu.CompilerParams(vmem_limit_bytes=VMEM_LIMIT),
        cost_estimate=pl.CostEstimate(
            flops=heads * 16 * rows * rows * HEAD,
            bytes_accessed=heads * rows * HEAD * 2 * 8,
            transcendentals=heads * 3 * rows * rows,
        ),
        name="attend",
    )(info, q, k, v, left, right)


def backward_kernel(first, info, q_ref, k_ref, v_ref, left_ref, right_ref, grad_ref, attn_ref, total_ref, *rest):
    dq_ref, own_ref, to_left_ref, to_right_ref = rest if first else rest[1:]
    q = q_ref[...]
    g = grad_ref[...]
    total = total_ref[0]
    delta = jnp.sum(g.astype(F32) * attn_ref[...].astype(F32), axis=0, keepdims=True)
    tiles = ((left_ref[0], left_ref[1]), (k_ref[...], v_ref[...]), (right_ref[0], right_ref[1]))
    live = (info[1] > 0, None, info[2] > 0)
    outs = (to_left_ref, own_ref, to_right_ref)
    dq = jnp.zeros((HEAD, q.shape[0]), F32)
    for j in range(3):
        k, v = tiles[j]
        if live[j] is None:
            factor, shift = LOG2_SCALE, total
        else:
            factor = jnp.where(live[j], LOG2_SCALE, 0.0)
            shift = jnp.where(live[j], total, FAR)
        w = jnp.exp2(nt(k, q) * factor - shift)
        outs[j][1] = nt(w.astype(BF), g).astype(outs[j].dtype)
        ds = (w * (nn(v, g) - delta)).astype(BF)
        outs[j][0] = (nn(ds, q) * SCALE).astype(outs[j].dtype)
        dq = dq + tn(k, ds)
    dq_ref[...] = (dq * SCALE).T.astype(BF)


def attend_back(info, q, k, v, left, right, grad, attn, total, heads, before):
    rows, cols = q.shape
    own = pl.BlockSpec((rows, HEAD), lambda h, info: (0, info[0] + h))
    side = pl.BlockSpec((2, rows, HEAD), lambda h, info: (0, 0, h))
    turned = pl.BlockSpec((HEAD, rows), lambda h, info: (h, 0))
    first = before is None
    return pl.pallas_call(
        functools.partial(backward_kernel, first),
        out_shape=(
            jax.ShapeDtypeStruct((rows, cols), BF),
            jax.ShapeDtypeStruct((2, rows, heads * HEAD), F32),
            jax.ShapeDtypeStruct((2, rows, heads * HEAD), BF),
            jax.ShapeDtypeStruct((2, rows, heads * HEAD), BF),
        ),
        grid_spec=pltpu.PrefetchScalarGridSpec(
            num_scalar_prefetch=1,
            grid=(heads,),
            in_specs=[own, own, own, side, side, turned, turned,
                      pl.BlockSpec((1, 1, rows), lambda h, info: (h, 0, 0))]
            + ([] if first else [pl.BlockSpec(memory_space=pl.ANY)]),
            out_specs=(own, side, side, side),
        ),
        input_output_aliases={} if first else {9: 0},
        compiler_params=pltpu.CompilerParams(vmem_limit_bytes=VMEM_LIMIT),
        cost_estimate=pl.CostEstimate(
            flops=heads * 40 * rows * rows * HEAD,
            bytes_accessed=heads * rows * HEAD * 2 * 16,
            transcendentals=heads * 3 * rows * rows,
        ),
        name="attend_back",
    )(info, q, k, v, left, right, grad, attn, total, *(() if first else (before,)))


def join_kernel(first, info, own_ref, a_ref, b_ref, *rest):
    dk_ref, dv_ref = rest if first else rest[2:]
    for i, out in enumerate((dk_ref, dv_ref)):
        out[...] = (own_ref[i] + a_ref[i].astype(F32) + b_ref[i].astype(F32)).astype(BF)


def join(info, own, a, b, heads, cols, before):
    rows = own.shape[1]
    side = pl.BlockSpec((2, rows, HEAD), lambda h, info: (0, 0, h))
    out = pl.BlockSpec((rows, HEAD), lambda h, info: (0, info[0] + h))
    first = before is None
    return pl.pallas_call(
        functools.partial(join_kernel, first),
        out_shape=(jax.ShapeDtypeStruct((rows, cols), BF),) * 2,
        grid_spec=pltpu.PrefetchScalarGridSpec(
            num_scalar_prefetch=1,
            grid=(heads,),
            in_specs=[side] * 3 + ([] if first else [pl.BlockSpec(memory_space=pl.ANY)] * 2),
            out_specs=(out, out),
        ),
        input_output_aliases={} if first else {4: 0, 5: 1},
        compiler_params=pltpu.CompilerParams(vmem_limit_bytes=VMEM_LIMIT),
        cost_estimate=pl.CostEstimate(
            flops=heads * 4 * rows * HEAD, bytes_accessed=heads * rows * HEAD * 20, transcendentals=0
        ),
        name="join",
    )(info, own, a, b, *(() if first else before))


def project_back_kernel(place, *refs):
    pieces, (u_ref, w_ref, g_ref, sems) = refs[:8], refs[8:]
    rows = pieces[0].shape[0]
    copies = []
    for i in range(8):
        spot = pl.multiple_of(place[i] * rows, rows)
        copies.append(pltpu.make_async_copy(pieces[i], w_ref.at[pl.ds(spot, rows)], sems.at[i]))
        copies[-1].start()
    for copy in copies:
        copy.wait()
    u = u_ref[...]

    def step(i, carry):
        spot = pl.ds(pl.multiple_of(i * 2 * rows, 2 * rows), 2 * rows)
        g_ref[spot, :] = nt(w_ref[spot, :], u).astype(BF)
        return carry

    lax.fori_loop(0, 4, step, 0)


def project_back(place, pieces, u):
    rows, wide = pieces[0].shape
    tokens = u.shape[0]
    whole = pl.BlockSpec(memory_space=pltpu.VMEM)
    return pl.pallas_call(
        project_back_kernel,
        out_shape=(
            jax.ShapeDtypeStruct((8 * rows, wide), BF),
            jax.ShapeDtypeStruct((8 * rows, tokens), BF),
        ),
        in_specs=[pl.BlockSpec(memory_space=pltpu.SMEM)] + [pl.BlockSpec(memory_space=pl.ANY)] * 8 + [whole],
        out_specs=(whole, whole),
        scratch_shapes=[pltpu.SemaphoreType.DMA((8,))],
        compiler_params=pltpu.CompilerParams(vmem_limit_bytes=VMEM_LIMIT),
        cost_estimate=pl.CostEstimate(
            flops=16 * rows * wide * tokens, bytes_accessed=40 * rows * wide, transcendentals=0
        ),
        name="project_back",
    )(place, *pieces, u)


def project_kernel(a_ref, b_ref, wa_ref, wb_ref, out_ref, turned):
    half = a_ref.shape[0]

    @pl.when(pl.program_id(0) == 0)
    def _():
        turned[:, :half] = a_ref[...].T
        turned[:, half:] = b_ref[...].T

    out_ref[...] = (nn(turned[:, :half], wa_ref[...]) + nn(turned[:, half:], wb_ref[...])).astype(BF)


def project(a, b, wa, wb):
    half, tokens = a.shape
    wide = wa.shape[1]
    block = 512
    side = pl.BlockSpec((half, tokens), lambda i: (0, 0))
    weight = pl.BlockSpec((half, block), lambda i: (0, i))
    return pl.pallas_call(
        project_kernel,
        out_shape=jax.ShapeDtypeStruct((tokens, wide), BF),
        grid=(wide // block,),
        in_specs=[side, side, weight, weight],
        out_specs=pl.BlockSpec((tokens, block), lambda i: (0, i)),
        scratch_shapes=[pltpu.VMEM((tokens, 2 * half), BF)],
        compiler_params=pltpu.CompilerParams(vmem_limit_bytes=VMEM_LIMIT),
        cost_estimate=pl.CostEstimate(
            flops=4 * half * wide * tokens, bytes_accessed=4 * half * wide + 2 * tokens * wide, transcendentals=0
        ),
        name="project",
    )(a, b, wa, wb)


def weight_grad_kernel(place, *refs):
    a_refs, u_refs, out_refs, total = refs[:4], refs[4:8], refs[8:12], refs[12]
    total[...] = sum(nn(a[...], u[...]) for a, u in zip(a_refs, u_refs)).astype(BF)
    rows = out_refs[0].shape[0]
    for i, out in enumerate(out_refs):
        out[...] = total[pl.ds(pl.multiple_of(place[i] * rows, rows), rows), :]


def weight_grad(place, a_list, u_list):
    rows, tokens = a_list[0].shape
    wide = u_list[0].shape[1]
    block = 512
    return pl.pallas_call(
        weight_grad_kernel,
        out_shape=(jax.ShapeDtypeStruct((rows // NZ, wide), BF),) * NZ,
        grid_spec=pltpu.PrefetchScalarGridSpec(
            num_scalar_prefetch=1,
            grid=(wide // block,),
            in_specs=[pl.BlockSpec((rows, tokens), lambda i, p: (0, 0))] * 4
            + [pl.BlockSpec((tokens, block), lambda i, p: (0, i))] * 4,
            out_specs=(pl.BlockSpec((rows // NZ, block), lambda i, p: (0, i)),) * NZ,
            scratch_shapes=[pltpu.VMEM((rows, block), BF)],
        ),
        compiler_params=pltpu.CompilerParams(vmem_limit_bytes=VMEM_LIMIT),
        cost_estimate=pl.CostEstimate(
            flops=8 * rows * wide * tokens, bytes_accessed=10 * tokens * wide, transcendentals=0
        ),
        name="weight_grad",
    )(place, *a_list, *u_list)


def place_kernel(spots, mine_ref, other_ref, out_ref):
    _, rows, cols = mine_ref.shape
    for j, ref in enumerate((mine_ref, other_ref)):
        top = pl.multiple_of(spots[4 + j] * rows, rows)
        for i in range(NY):
            start = pl.multiple_of(spots[i] * cols, cols)
            out_ref[pl.ds(top, rows), pl.ds(start, cols)] = ref[i].astype(F32)


def place_pieces(spots, mine, other):
    _, rows, cols = mine.shape
    whole = pl.BlockSpec(memory_space=pltpu.VMEM)
    return pl.pallas_call(
        place_kernel,
        out_shape=jax.ShapeDtypeStruct((2 * rows, NY * cols), F32),
        in_specs=[pl.BlockSpec(memory_space=pltpu.SMEM), whole, whole],
        out_specs=whole,
        name="place_pieces",
    )(spots, mine, other)


def add(*terms):
    return functools.reduce(lambda s, t: s + t.astype(F32), terms[1:], terms[0].astype(F32))


def on_device(query, key_in, value_in, out_weight, grad_out, neighbours):
    q, k, v, upstream = query[0], key_in[0], value_in[0], grad_out[0]
    rows, cols = q.shape
    half = cols // 2
    heads = half // HEAD
    dp = lax.axis_index("dp")
    tile = lax.axis_index("space")
    a, z, c = dp // (NZ * NC), (dp // NC) % NZ, dp % NC
    lo, y = tile // NY, tile % NY

    own_list = neighbours[tile]
    live_left = jnp.any((own_list == tile - 1) & (own_list >= 0)).astype(jnp.int32)
    live_right = jnp.any(own_list == tile + 1).astype(jnp.int32)
    infos = [
        jnp.stack([part * heads, live_left, live_right]).astype(jnp.int32) for part in (a, 1 - a)
    ]

    near = []
    for part in (a, 1 - a):
        pair = jnp.stack(
            [lax.dynamic_slice_in_dim(t, part * half, half, axis=1) for t in (k, v)]
        )
        near.append((to_next(pair), to_previous(pair)))

    w0 = [out_weight] + [move_z(out_weight, i) for i in (1, 3, 2)]
    cross = move_cross(out_weight)
    w1 = [cross] + [move_z(cross, i) for i in (1, 3)] + [move_cross(w0[3])]
    z_of = [z, (z + 3) % NZ, (z + 1) % NZ, (z + 2) % NZ]
    place = jnp.stack([2 * i + c for i in z_of] + [2 * i + 1 - c for i in z_of]).astype(jnp.int32)

    up_core = move_core(upstream)
    up_lo = move_lo(upstream)
    up_both = move_core(up_lo)

    attns, owns, back_sends, weights = [], [], [], []
    dq = None
    for part, w, info, (left, right) in zip((0, 1), (w0, w1), infos, near):
        attn, total = attend(info, q, k, v, left, right, heads)
        w_full, grad = project_back(place, w + [move_core(t) for t in w], upstream)
        dq, own, to_left, to_right = attend_back(
            info, q, k, v, left, right, grad, attn, total, heads, dq
        )
        back_sends.append((to_next(to_right), to_previous(to_left)))
        attns.append(attn)
        owns.append(own)
        weights.append(w_full)

    mixed = project(attns[0], attns[1], weights[0], weights[1])

    z_place = jnp.stack([(z + i) % NZ for i in range(NZ)]).astype(jnp.int32)
    u_list = [upstream, up_core, up_lo, up_both]
    sums = []
    for attn in attns:
        parts = attn.reshape(NZ, NC, NL, -1, rows)
        sub = parts.shape[3]

        def pick(core, low):
            return lax.dynamic_slice(
                parts, (0, core, low, 0, 0), (NZ, 1, 1, sub, rows)
            ).reshape(NZ * sub, rows)

        a_list = [
            pick(c, lo),
            move_core(pick(1 - c, lo)),
            move_lo(pick(c, 1 - lo)),
            move_lo_core(pick(1 - c, 1 - lo)),
        ]
        pieces = weight_grad(z_place, a_list, u_list)
        sums.append(add(pieces[0], *[move_z(pieces[i], i) for i in (1, 3, 2)]))
    both = sums[0] + move_hi(sums[1].astype(BF)).astype(F32)
    quarter = both.shape[1] // NY
    both = both.astype(BF)

    def column(i):
        return lax.dynamic_slice_in_dim(both, ((y + i) % NY) * quarter, quarter, axis=1)

    mine = add(column(0), *[move_y(column(i), i) for i in (1, 3, 2)]).astype(BF)
    mine = jnp.stack([mine] + [move_y(mine, i) for i in (1, 2, 3)])
    other = move_lo(mine)
    spots = jnp.stack([(y - i) % NY for i in range(NY)] + [lo, 1 - lo]).astype(jnp.int32)
    grad_weight = place_pieces(spots, mine, other)

    done = None
    for own, (from_left, from_right), info in zip(owns, back_sends, infos):
        done = join(info, own, from_left, from_right, heads, cols, done)
    dk, dv = done
    return (mixed[None], dq[None], dk[None], dv[None], grad_weight)


def solution(mesh):
    return jax.shard_map(
        on_device,
        mesh=mesh,
        in_specs=(
            P("dp", "space", None),
            P("dp", "space", None),
            P("dp", "space", None),
            P("dp", None),
            P("dp", "space", None),
            P(),
        ),
        out_specs=(
            P("dp", "space", None),
            P("dp", "space", None),
            P("dp", "space", None),
            P("dp", "space", None),
            P("dp", None),
        ),
        check_vma=False,
    )
```

```python
import functools
import math

import jax
import jax.numpy as jnp
from jax import lax
from jax.experimental import pallas as pl
from jax.experimental.pallas import tpu as pltpu
from jax.sharding import PartitionSpec as P

HEAD = 128
SCALE = 1.0 / math.sqrt(HEAD)
LOG2_SCALE = SCALE * math.log2(math.e)
FAR = 1e30
COST = pl.CostEstimate(flops=1000, bytes_accessed=1000, transcendentals=0)
BF = jnp.bfloat16
F32 = jnp.float32
VMEM_LIMIT = 24 * 1024 * 1024

NX, NZ, NC, NL, NY = 2, 4, 2, 2, 4
NS = NL * NY


def moves(change):
    pairs = []
    for a in range(NX):
        for z in range(NZ):
            for c in range(NC):
                for l in range(NL):
                    for y in range(NY):
                        b, w, d, m, v = change(a, z, c, l, y)
                        src = ((a * NZ + z) * NC + c) * NS + l * NY + y
                        dst = ((b * NZ + w) * NC + d) * NS + m * NY + v
                        pairs.append((src, dst))
    return pairs


def move(x, change):
    return lax.ppermute(x, ("dp", "space"), moves(change))


def move_core(x):
    return move(x, lambda a, z, c, l, y: (a, z, 1 - c, l, y))


def move_lo(x):
    return move(x, lambda a, z, c, l, y: (a, z, c, 1 - l, y))


def move_lo_core(x):
    return move(x, lambda a, z, c, l, y: (a, z, 1 - c, 1 - l, y))


def move_hi(x):
    return move(x, lambda a, z, c, l, y: (1 - a, z, c, l, y))


def move_cross(x):
    return move(x, lambda a, z, c, l, y: (1 - a, z, c, 1 - l, y))


def move_cross_core(x):
    return move(x, lambda a, z, c, l, y: (1 - a, z, 1 - c, 1 - l, y))


def move_z(x, k):
    return move(x, lambda a, z, c, l, y: (a, (z + k) % NZ, c, l, y))


def move_y(x, k):
    return move(x, lambda a, z, c, l, y: (a, z, c, l, (y + k) % NY))


def to_next(x):
    return lax.ppermute(x, "space", [(i, i + 1) for i in range(NS - 1)])


def to_previous(x):
    return lax.ppermute(x, "space", [(i + 1, i) for i in range(NS - 1)])


def nt(a, b):
    return lax.dot_general(a, b, (((1,), (1,)), ((), ())), preferred_element_type=F32)


def tn(a, b):
    return lax.dot_general(a, b, (((0,), (0,)), ((), ())), preferred_element_type=F32)


def nn(a, b):
    return lax.dot_general(a, b, (((1,), (0,)), ((), ())), preferred_element_type=F32)


PER_F = 2
PER_B = 2


def windows(live, shift):
    factors = [jnp.where(on, LOG2_SCALE, 0.0) for on in live]
    return factors, [jnp.where(on, shift, FAR) for on in live]


def forward_head(live, cols, q_ref, k_ref, v_ref, left_ref, right_ref):
    q = q_ref[:, cols]
    keys = (left_ref[0, :, cols], k_ref[:, cols], right_ref[0, :, cols])
    values = (left_ref[1, :, cols], v_ref[:, cols], right_ref[1, :, cols])
    scores = [nt(k, q) for k in keys]
    tops = [jnp.max(s, axis=0, keepdims=True) for s in scores]
    top = tops[1]
    for j in (0, 2):
        top = jnp.maximum(top, jnp.where(live[j // 2], tops[j], -FAR))
    top = top * LOG2_SCALE
    total = jnp.zeros_like(top)
    acc = jnp.zeros((HEAD, q.shape[0]), F32)
    for j in range(3):
        factor = LOG2_SCALE if j == 1 else jnp.where(live[j // 2], LOG2_SCALE, 0.0)
        shift = top if j == 1 else jnp.where(live[j // 2], top, FAR)
        p = jnp.exp2(scores[j] * factor - shift)
        total = total + jnp.sum(p, axis=0, keepdims=True)
        acc = acc + tn(values[j], p.astype(BF))
    return (acc / total).astype(BF), top + jnp.log2(total)


def forward_kernel(per, info, q_ref, k_ref, v_ref, left_ref, right_ref, *rest):
    attn_ref, total_ref = rest[-2:]
    live = (info[1] > 0, info[2] > 0)
    for i in range(per):
        cols = slice(i * HEAD, (i + 1) * HEAD)
        attn_ref[cols, :], total_ref[i] = forward_head(
            live, cols, q_ref, k_ref, v_ref, left_ref, right_ref
        )


def attend(info, q, k, v, left, right, heads, before=()):
    rows = q.shape[0]
    per = PER_F
    own = pl.BlockSpec((rows, per * HEAD), lambda h, info: (0, info[0] // per + h))
    side = pl.BlockSpec((2, rows, per * HEAD), lambda h, info: (0, 0, h))
    return pl.pallas_call(
        functools.partial(forward_kernel, per),
        out_shape=(
            jax.ShapeDtypeStruct((heads * HEAD, rows), BF),
            jax.ShapeDtypeStruct((heads, 1, rows), F32),
        ),
        grid_spec=pltpu.PrefetchScalarGridSpec(
            num_scalar_prefetch=1,
            grid=(heads // per,),
            in_specs=[own, own, own, side, side] + [pl.BlockSpec(memory_space=pl.ANY)] * len(before),
            out_specs=(
                pl.BlockSpec((per * HEAD, rows), lambda h, info: (h, 0)),
                pl.BlockSpec((per, 1, rows), lambda h, info: (h, 0, 0)),
            ),
        ),
        compiler_params=pltpu.CompilerParams(vmem_limit_bytes=VMEM_LIMIT),
        cost_estimate=COST,
        name="attend",
    )(info, q, k, v, left, right, *before)


def backward_kernel(per, info, q_ref, k_ref, v_ref, left_ref, right_ref, grad_ref, attn_ref, total_ref, *rest):
    dq_ref, own_ref, to_left_ref, to_right_ref = rest[-4:]
    outs = (to_left_ref, own_ref, to_right_ref)
    live = (info[1] > 0, info[2] > 0)
    for i in range(per):
        cols = slice(i * HEAD, (i + 1) * HEAD)
        q = q_ref[:, cols]
        g = grad_ref[cols, :]
        total = total_ref[i]
        delta = jnp.sum(g.astype(F32) * attn_ref[cols, :].astype(F32), axis=0, keepdims=True)
        keys = (left_ref[0, :, cols], k_ref[:, cols], right_ref[0, :, cols])
        values = (left_ref[1, :, cols], v_ref[:, cols], right_ref[1, :, cols])
        dq = jnp.zeros((HEAD, q.shape[0]), F32)
        for j in range(3):
            k, v = keys[j], values[j]
            factor = LOG2_SCALE if j == 1 else jnp.where(live[j // 2], LOG2_SCALE, 0.0)
            shift = total if j == 1 else jnp.where(live[j // 2], total, FAR)
            w = jnp.exp2(nt(k, q) * factor - shift)
            outs[j][1, :, cols] = nt(w.astype(BF), g).astype(BF)
            ds = (w * (nn(v, g) - delta)).astype(BF)
            outs[j][0, :, cols] = (nn(ds, q) * SCALE).astype(BF)
            dq = dq + tn(k, ds)
        dq_ref[:, cols] = (dq * SCALE).T.astype(BF)


def attend_back(info, q, k, v, left, right, grad, attn, total, heads, before, again):
    rows, cols = q.shape
    per = PER_B
    own = pl.BlockSpec((rows, per * HEAD), lambda h, info: (0, info[0] // per + h))
    side = pl.BlockSpec((2, rows, per * HEAD), lambda h, info: (0, 0, h))
    turned = pl.BlockSpec((per * HEAD, rows), lambda h, info: (h, 0))
    return pl.pallas_call(
        functools.partial(backward_kernel, per),
        out_shape=(jax.ShapeDtypeStruct((rows, cols), BF),)
        + (jax.ShapeDtypeStruct((2, rows, heads * HEAD), BF),) * 3,
        grid_spec=pltpu.PrefetchScalarGridSpec(
            num_scalar_prefetch=1,
            grid=(heads // per,),
            in_specs=[own, own, own, side, side, turned, turned,
                      pl.BlockSpec((per, 1, rows), lambda h, info: (h, 0, 0))]
            + [pl.BlockSpec(memory_space=pl.ANY)] * len(before),
            out_specs=(own, side, side, side),
        ),
        input_output_aliases={9: 0} if again else {},
        compiler_params=pltpu.CompilerParams(vmem_limit_bytes=VMEM_LIMIT),
        cost_estimate=COST,
        name="attend_back",
    )(info, q, k, v, left, right, grad, attn, total, *before)


JOIN_ROWS = 192


def join_kernel(first, info, own_ref, a_ref, b_ref, *rest):
    dk_ref, dv_ref = rest if first else rest[2:]
    for i, out in enumerate((dk_ref, dv_ref)):
        out[...] = (own_ref[i].astype(F32) + a_ref[i].astype(F32) + b_ref[i].astype(F32)).astype(BF)


def join(info, own, a, b, heads, cols, before):
    rows = own.shape[1]
    wide = heads * HEAD
    side = pl.BlockSpec((2, JOIN_ROWS, wide), lambda r, info: (0, r, 0))
    out = pl.BlockSpec((JOIN_ROWS, wide), lambda r, info: (r, info[0] // heads))
    first = before is None
    return pl.pallas_call(
        functools.partial(join_kernel, first),
        out_shape=(jax.ShapeDtypeStruct((rows, cols), BF),) * 2,
        grid_spec=pltpu.PrefetchScalarGridSpec(
            num_scalar_prefetch=1,
            grid=(rows // JOIN_ROWS,),
            in_specs=[side] * 3 + ([] if first else [pl.BlockSpec(memory_space=pl.ANY)] * 2),
            out_specs=(out, out),
        ),
        input_output_aliases={} if first else {4: 0, 5: 1},
        compiler_params=pltpu.CompilerParams(vmem_limit_bytes=VMEM_LIMIT),
        cost_estimate=COST,
        name="join",
    )(info, own, a, b, *(() if first else before))


def hold_kernel(x_ref, *rest):
    del x_ref, rest


def hold(x, *before):
    anywhere = pl.BlockSpec(memory_space=pl.ANY)
    return pl.pallas_call(
        hold_kernel,
        out_shape=jax.ShapeDtypeStruct(x.shape, x.dtype),
        in_specs=[anywhere] * (1 + len(before)),
        out_specs=anywhere,
        input_output_aliases={0: 0},
        cost_estimate=COST,
        name="hold",
    )(x, *before)


def window_kernel(info, k_ref, v_ref, *rest):
    rest[-1][0] = k_ref[...]
    rest[-1][1] = v_ref[...]


def window(info, k, v, heads, before=()):
    rows = k.shape[0]
    wide = heads * HEAD
    block = pl.BlockSpec((rows // 2, wide), lambda r, info: (r, info[0] // heads))
    return pl.pallas_call(
        window_kernel,
        out_shape=jax.ShapeDtypeStruct((2, rows, wide), BF),
        grid_spec=pltpu.PrefetchScalarGridSpec(
            num_scalar_prefetch=1,
            grid=(2,),
            in_specs=[block, block] + [pl.BlockSpec(memory_space=pl.ANY)] * len(before),
            out_specs=pl.BlockSpec((2, rows // 2, wide), lambda r, info: (0, r, 0)),
        ),
        compiler_params=pltpu.CompilerParams(vmem_limit_bytes=VMEM_LIMIT),
        cost_estimate=COST,
        name="window",
    )(info, k, v, *before)


def project_back_kernel(place, *refs):
    pieces, (u_ref, other_ref) = refs[:NZ], refs[NZ:NZ + 2]
    mine_ref, theirs_ref, w = refs[-3:]
    rows = pieces[0].shape[0]
    for i, piece in enumerate(pieces):
        w[pl.ds(pl.multiple_of(place[i] * rows, rows), rows), :] = piece[...]
    mine_ref[...] = nt(w[...], u_ref[...]).astype(BF)
    theirs_ref[...] = nt(w[...], other_ref[...]).astype(BF)


def project_back(place, pieces, u, other, before=()):
    rows, wide = pieces[0].shape
    tokens = u.shape[0]
    whole = pl.BlockSpec(memory_space=pltpu.VMEM)
    return pl.pallas_call(
        project_back_kernel,
        out_shape=(jax.ShapeDtypeStruct((NZ * rows, tokens), BF),) * 2,
        in_specs=[pl.BlockSpec(memory_space=pltpu.SMEM)] + [whole] * (NZ + 2)
        + [pl.BlockSpec(memory_space=pl.ANY)] * len(before),
        out_specs=(whole, whole),
        scratch_shapes=[pltpu.VMEM((NZ * rows, wide), BF)],
        compiler_params=pltpu.CompilerParams(vmem_limit_bytes=VMEM_LIMIT),
        cost_estimate=COST,
        name="project_back",
    )(place, *pieces, u, other, *before)


SPLIT = 2


def project_kernel(adds, place, a_ref, b_ref, *refs):
    pieces, sent = refs[:2 * NZ], refs[2 * NZ:2 * NZ + adds]
    outs, w = refs[-1 - (1 if adds else SPLIT):-1], refs[-1]
    rows = pieces[0].shape[0]
    half = NZ * rows
    for i, piece in enumerate(pieces):
        spot = (i // NZ) * half + place[i % NZ] * rows
        w[pl.ds(pl.multiple_of(spot, rows), rows), :] = piece[...]
    block = w.shape[1] // SPLIT
    first, second = a_ref[...].T, b_ref[...].T
    for i in range(SPLIT):
        cols = slice(i * block, (i + 1) * block)
        total = nn(first, w[:half, cols]) + nn(second, w[half:, cols])
        if adds:
            outs[0][:, cols] = (total + sent[i][...].astype(F32)).astype(BF)
        else:
            outs[i][...] = total.astype(BF)


def project(place, a, b, pieces, sent, before=()):
    tokens = a.shape[1]
    rows, wide = pieces[0].shape
    whole = pl.BlockSpec(memory_space=pltpu.VMEM)
    if sent:
        out_shape = (jax.ShapeDtypeStruct((tokens, wide), BF),)
    else:
        out_shape = (jax.ShapeDtypeStruct((tokens, wide // SPLIT), BF),) * SPLIT
    return pl.pallas_call(
        functools.partial(project_kernel, len(sent)),
        out_shape=out_shape,
        in_specs=[pl.BlockSpec(memory_space=pltpu.SMEM)] + [whole] * (2 + 2 * NZ + len(sent))
        + [pl.BlockSpec(memory_space=pl.ANY)] * len(before),
        out_specs=(whole,) * len(out_shape),
        scratch_shapes=[pltpu.VMEM((2 * NZ * rows, wide), BF)],
        compiler_params=pltpu.CompilerParams(vmem_limit_bytes=32 * 1024 * 1024),
        cost_estimate=COST,
        name="project",
    )(place, a, b, *pieces, *sent, *before)


def weight_grad_kernel(place, *refs):
    a_refs, u_refs, half_refs = refs[:4], refs[4:6], refs[6:10]
    out_refs, total = refs[-1 - NZ:-1], refs[-1]
    near = sum(nn(a[...], u[...]) for a, u in zip(a_refs, u_refs))
    for i in range(2):

        @pl.when(pl.program_id(0) == i)
        def _():
            far = sum(nn(a[...], u[...]) for a, u in zip(a_refs[2:], half_refs[2 * i:]))
            total[...] = (near + far).astype(BF)

    rows = out_refs[0].shape[0]
    for i, out in enumerate(out_refs):
        out[...] = total[pl.ds(pl.multiple_of(place[i] * rows, rows), rows), :]


def weight_grad(place, a_list, u, core, first, second, before):
    rows, tokens = a_list[0].shape
    wide = u.shape[1]
    block = wide // 2
    sub = rows // NZ
    return pl.pallas_call(
        weight_grad_kernel,
        out_shape=(jax.ShapeDtypeStruct((sub, wide), BF),) * NZ,
        grid_spec=pltpu.PrefetchScalarGridSpec(
            num_scalar_prefetch=1,
            grid=(wide // block,),
            in_specs=[pl.BlockSpec((rows, tokens), lambda i, p: (0, 0))] * 4
            + [pl.BlockSpec((tokens, block), lambda i, p: (0, i))] * 2
            + [pl.BlockSpec((tokens, block), lambda i, p: (0, 0))] * 4
            + [pl.BlockSpec(memory_space=pl.ANY)] * len(before),
            out_specs=(pl.BlockSpec((sub, block), lambda i, p: (0, i)),) * NZ,
            scratch_shapes=[pltpu.VMEM((rows, block), BF)],
        ),
        compiler_params=pltpu.CompilerParams(vmem_limit_bytes=32 * 1024 * 1024),
        cost_estimate=COST,
        name="weight_grad",
    )(place, *a_list, u, core, *first, *second, *before)


def place_kernel(spots, *refs):
    out_ref = refs[-1]
    wide = refs[0].shape[1]
    for j, ref in enumerate(refs[:-1]):
        out_ref[:, pl.ds(pl.multiple_of(spots[j] * wide, wide), wide)] = ref[...].astype(F32)


def place_columns(spots, *pieces):
    rows, cols = pieces[0].shape
    whole = pl.BlockSpec(memory_space=pltpu.VMEM)
    return pl.pallas_call(
        place_kernel,
        out_shape=jax.ShapeDtypeStruct((rows, len(pieces) * cols), F32),
        in_specs=[pl.BlockSpec(memory_space=pltpu.SMEM)] + [whole] * len(pieces),
        out_specs=whole,
        cost_estimate=COST,
        name="place_columns",
    )(spots, *pieces)


def add(*terms):
    return functools.reduce(lambda s, t: s + t.astype(F32), terms[1:], terms[0].astype(F32))


def on_device(query, key_in, value_in, out_weight, grad_out, neighbours):
    q, k, v, upstream = query[0], key_in[0], value_in[0], grad_out[0]
    rows, cols = q.shape
    half = cols // 2
    heads = half // HEAD
    dp = lax.axis_index("dp")
    tile = lax.axis_index("space")
    a, z, c = dp // (NZ * NC), (dp // NC) % NZ, dp % NC
    lo, y = tile // NY, tile % NY

    own_list = neighbours[tile]
    live_left = jnp.any((own_list == tile - 1) & (own_list >= 0)).astype(jnp.int32)
    live_right = jnp.any(own_list == tile + 1).astype(jnp.int32)
    infos = [
        jnp.stack([part * heads, live_left, live_right]).astype(jnp.int32) for part in (a, 1 - a)
    ]

    sides = [jnp.full((1,), part * heads, jnp.int32) for part in (a, 1 - a)]
    pair = window(sides[0], k, v, heads)
    near0 = (to_next(pair), to_previous(pair))
    pair = window(sides[1], k, v, heads, near0)
    near1 = (to_next(pair), to_previous(pair))

    def around(x):
        up, down = move_z(x, 1), move_z(x, 3)
        return [x, up, down, move_z(up, 1)]

    cross = move_cross(out_weight)
    w0 = around(out_weight)
    place = jnp.stack([z, (z + 3) % NZ, (z + 1) % NZ, (z + 2) % NZ]).astype(jnp.int32)

    middle = upstream.shape[1] // 2
    up_core = move_core(upstream)
    cross_first = move_cross(hold(upstream[:, :middle], cross))
    cross_second = move_cross(hold(upstream[:, middle:], cross_first))

    def back(w, before):
        mine, theirs = project_back(place, w, upstream, up_core, before)
        both = (mine.reshape(NZ, -1, rows), move_core(theirs).reshape(NZ, -1, rows))
        both = jnp.where(c == 0, jnp.stack(both, axis=1), jnp.stack(both[::-1], axis=1))
        return both.reshape(half, rows)

    attn0, total0 = attend(infos[0], q, k, v, *near0, heads)
    w1 = around(hold(cross, attn0))
    grad0 = back(w0, (attn0,))
    attn1, total1 = attend(infos[1], q, k, v, *near1, heads, (grad0,))
    dq, own0, to_left, to_right = attend_back(
        infos[0], q, k, v, *near0, grad0, attn0, total0, heads, (attn1,), False
    )
    sent0 = (to_next(to_right), to_previous(to_left))

    def pick(attn, core):
        parts = attn.reshape(NZ, NC, -1, rows)
        sub = parts.shape[2]
        return lax.dynamic_slice(parts, (0, core, 0, 0), (NZ, 1, sub, rows)).reshape(
            NZ * sub, rows
        )

    own_part, core_part = pick(attn1, c), pick(attn1, 1 - c)
    a_list = [
        pick(attn0, c),
        move_core(pick(attn0, 1 - c)),
        move_cross(own_part),
        move_cross_core(core_part),
    ]
    grad1 = back(w1, (own0,))
    core_far = move_core(core_part)
    dq, own1, to_left, to_right = attend_back(
        infos[1], q, k, v, *near1, grad1, attn1, total1, heads, (dq, core_far), True
    )
    sent1 = (to_next(to_right), to_previous(to_left))
    z_place = jnp.stack([(z + i) % NZ for i in range(NZ)]).astype(jnp.int32)
    pieces = weight_grad(
        z_place, a_list, upstream, up_core, (cross_first, move_core(cross_first)),
        (cross_second, move_core(cross_second)), (own1,) + sent0,
    )
    theirs = project(place, a_list[1], core_far, w0 + w1, (), pieces[:1])
    sent = tuple(move_core(t) for t in theirs)
    (mixed,) = project(place, a_list[0], own_part, w0 + w1, sent)
    done = join(infos[0], own0, *sent0, heads, cols, None)
    done = join(infos[1], own1, *sent1, heads, cols, done)

    sums = add(hold(pieces[0], *done), *[move_z(pieces[i], i) for i in (1, 3, 2)])
    quarter = sums.shape[1] // NY

    def column(i):
        return lax.dynamic_slice_in_dim(sums, ((y + i) % NY) * quarter, quarter, axis=1)

    mine = add(column(0), *[move_y(column(i).astype(BF), i) for i in (1, 3, 2)]).astype(BF)
    mine = hold(mine, mixed)
    mine = add(mine, move_lo(mine)).astype(BF)
    spots = jnp.stack([(y - i) % NY for i in (0, 1, 3, 2)]).astype(jnp.int32)
    grad_weight = place_columns(spots, mine, *[move_y(mine, i) for i in (1, 3, 2)])
    dk, dv = done
    return (mixed[None], dq[None], dk[None], dv[None], grad_weight)


def solution(mesh):
    return jax.shard_map(
        on_device,
        mesh=mesh,
        in_specs=(
            P("dp", "space", None),
            P("dp", "space", None),
            P("dp", "space", None),
            P("dp", None),
            P("dp", "space", None),
            P(),
        ),
        out_specs=(
            P("dp", "space", None),
            P("dp", "space", None),
            P("dp", "space", None),
            P("dp", "space", None),
            P("dp", None),
        ),
        check_vma=False,
    )
```

```python
import functools
import math

import jax
import jax.numpy as jnp
from jax import lax
from jax.experimental import pallas as pl
from jax.experimental.pallas import tpu as pltpu
from jax.sharding import PartitionSpec as P

HEAD = 128
SCALE = 1.0 / math.sqrt(HEAD)
LOG2_SCALE = SCALE * math.log2(math.e)
FAR = 1e30
TILE_AT, CORE_AT, FROM_Z, TO_Z, TO_Y, FROM_Y, AROUND = 2, 3, 4, 8, 12, 16, 20
SLOTS = 3
COST = pl.CostEstimate(flops=1000, bytes_accessed=1000, transcendentals=0)
BF = jnp.bfloat16
F32 = jnp.float32
VMEM_LIMIT = 60 * 1024 * 1024
WG_STEPS = 4

NX, NZ, NC, NL, NY = 2, 4, 2, 2, 4
NS = NL * NY


def moves(change):
    pairs = []
    for a in range(NX):
        for z in range(NZ):
            for c in range(NC):
                for l in range(NL):
                    for y in range(NY):
                        b, w, d, m, v = change(a, z, c, l, y)
                        src = ((a * NZ + z) * NC + c) * NS + l * NY + y
                        dst = ((b * NZ + w) * NC + d) * NS + m * NY + v
                        pairs.append((src, dst))
    return pairs


def move(x, change):
    return lax.ppermute(x, ("dp", "space"), moves(change))


def move_core(x):
    return move(x, lambda a, z, c, l, y: (a, z, 1 - c, l, y))


def move_lo(x):
    return move(x, lambda a, z, c, l, y: (a, z, c, 1 - l, y))


def move_lo_core(x):
    return move(x, lambda a, z, c, l, y: (a, z, 1 - c, 1 - l, y))


def move_hi(x):
    return move(x, lambda a, z, c, l, y: (1 - a, z, c, l, y))


def move_cross(x):
    return move(x, lambda a, z, c, l, y: (1 - a, z, c, 1 - l, y))


def move_cross_core(x):
    return move(x, lambda a, z, c, l, y: (1 - a, z, 1 - c, 1 - l, y))


def move_z(x, k):
    return move(x, lambda a, z, c, l, y: (a, (z + k) % NZ, c, l, y))


def move_y(x, k):
    return move(x, lambda a, z, c, l, y: (a, z, c, l, (y + k) % NY))


def to_next(x):
    return lax.ppermute(x, "space", [(i, i + 1) for i in range(NS - 1)])


def to_previous(x):
    return lax.ppermute(x, "space", [(i + 1, i) for i in range(NS - 1)])


def nt(a, b):
    return lax.dot_general(a, b, (((1,), (1,)), ((), ())), preferred_element_type=F32)


def tn(a, b):
    return lax.dot_general(a, b, (((0,), (0,)), ((), ())), preferred_element_type=F32)


def nn(a, b):
    return lax.dot_general(a, b, (((1,), (0,)), ((), ())), preferred_element_type=F32)


PER_F = 2
PER_B = 2


def windows(live, shift):
    factors = [jnp.where(on, LOG2_SCALE, 0.0) for on in live]
    return factors, [jnp.where(on, shift, FAR) for on in live]


def forward_head(live, cols, q_ref, k_ref, v_ref, left_ref, right_ref):
    q = q_ref[:, cols]
    keys = (left_ref[0, :, cols], k_ref[:, cols], right_ref[0, :, cols])
    values = (left_ref[1, :, cols], v_ref[:, cols], right_ref[1, :, cols])
    scores = [nt(k, q) for k in keys]
    tops = [jnp.max(s, axis=0, keepdims=True) for s in scores]
    top = tops[1]
    for j in (0, 2):
        top = jnp.maximum(top, jnp.where(live[j // 2], tops[j], -FAR))
    top = top * LOG2_SCALE
    total = jnp.zeros_like(top)
    acc = jnp.zeros((HEAD, q.shape[0]), F32)
    for j in range(3):
        factor = LOG2_SCALE if j == 1 else jnp.where(live[j // 2], LOG2_SCALE, 0.0)
        shift = top if j == 1 else jnp.where(live[j // 2], top, FAR)
        p = jnp.exp2(scores[j] * factor - shift)
        total = total + jnp.sum(p, axis=0, keepdims=True)
        acc = acc + tn(values[j], p.astype(BF))
    return (acc / total).astype(BF), top + jnp.log2(total)


def live_sides(info):
    tile = info[TILE_AT]
    found = [jnp.zeros((), jnp.bool_)] * 2
    for i in range(SLOTS):
        entry = info[AROUND + SLOTS * tile + i]
        found = [on | ((entry == tile + d) & (entry >= 0)) for on, d in zip(found, (-1, 1))]
    return found


def forward_kernel(per, part, info, q_ref, k_ref, v_ref, left_ref, right_ref, *rest):
    attn_ref, total_ref = rest[-2:]
    live = live_sides(info)
    for i in range(per):
        cols = slice(i * HEAD, (i + 1) * HEAD)
        attn_ref[cols, :], total_ref[i] = forward_head(
            live, cols, q_ref, k_ref, v_ref, left_ref, right_ref
        )


def attend(part, info, q, k, v, left, right, heads, before=()):
    rows = q.shape[0]
    per = PER_F
    own = pl.BlockSpec((rows, per * HEAD), lambda h, info: (0, info[part] // per + h))
    side = pl.BlockSpec((2, rows, per * HEAD), lambda h, info: (0, 0, h))
    return pl.pallas_call(
        functools.partial(forward_kernel, per, part),
        out_shape=(
            jax.ShapeDtypeStruct((heads * HEAD, rows), BF),
            jax.ShapeDtypeStruct((heads, 1, rows), F32),
        ),
        grid_spec=pltpu.PrefetchScalarGridSpec(
            num_scalar_prefetch=1,
            grid=(heads // per,),
            in_specs=[own, own, own, side, side] + [pl.BlockSpec(memory_space=pl.ANY)] * len(before),
            out_specs=(
                pl.BlockSpec((per * HEAD, rows), lambda h, info: (h, 0)),
                pl.BlockSpec((per, 1, rows), lambda h, info: (h, 0, 0)),
            ),
        ),
        compiler_params=pltpu.CompilerParams(vmem_limit_bytes=VMEM_LIMIT),
        cost_estimate=COST,
        name="attend",
    )(info, q, k, v, left, right, *before)


def backward_kernel(per, part, info, q_ref, k_ref, v_ref, left_ref, right_ref, mine_ref, theirs_ref, attn_ref, total_ref, *rest):
    dq_ref, own_ref, to_left_ref, to_right_ref, grad_ref = rest[-5:]
    step = pl.program_id(0)

    @pl.when(step == 0)
    def _():
        size = mine_ref.shape[0] // NZ
        for i in range(NZ):
            for ref, core in ((mine_ref, info[CORE_AT]), (theirs_ref, 1 - info[CORE_AT])):
                spot = pl.multiple_of((NC * i + core) * size, size)
                grad_ref[pl.ds(spot, size), :] = ref[i * size:(i + 1) * size, :]

    outs = (to_left_ref, own_ref, to_right_ref)
    live = live_sides(info)
    for i in range(per):
        cols = slice(i * HEAD, (i + 1) * HEAD)
        q = q_ref[:, cols]
        here = pl.multiple_of((step * per + i) * HEAD, HEAD)
        g = grad_ref[pl.ds(here, HEAD), :]
        total = total_ref[i]
        delta = jnp.sum(g.astype(F32) * attn_ref[cols, :].astype(F32), axis=0, keepdims=True)
        keys = (left_ref[0, :, cols], k_ref[:, cols], right_ref[0, :, cols])
        values = (left_ref[1, :, cols], v_ref[:, cols], right_ref[1, :, cols])
        dq = jnp.zeros((HEAD, q.shape[0]), F32)
        for j in range(3):
            k, v = keys[j], values[j]
            factor = LOG2_SCALE if j == 1 else jnp.where(live[j // 2], LOG2_SCALE, 0.0)
            shift = total if j == 1 else jnp.where(live[j // 2], total, FAR)
            w = jnp.exp2(nt(k, q) * factor - shift)
            outs[j][1, :, cols] = nt(w.astype(BF), g).astype(BF)
            ds = (w * (nn(v, g) - delta)).astype(BF)
            outs[j][0, :, cols] = (nn(ds, q) * SCALE).astype(BF)
            dq = dq + tn(k, ds)
        dq_ref[:, cols] = (dq * SCALE).T.astype(BF)


def attend_back(part, info, q, k, v, left, right, grads, attn, total, heads, before, again):
    rows, cols = q.shape
    per = PER_B
    own = pl.BlockSpec((rows, per * HEAD), lambda h, info: (0, info[part] // per + h))
    side = pl.BlockSpec((2, rows, per * HEAD), lambda h, info: (0, 0, h))
    turned = pl.BlockSpec((per * HEAD, rows), lambda h, info: (h, 0))
    return pl.pallas_call(
        functools.partial(backward_kernel, per, part),
        out_shape=(jax.ShapeDtypeStruct((rows, cols), BF),)
        + (jax.ShapeDtypeStruct((2, rows, heads * HEAD), BF),) * 3,
        grid_spec=pltpu.PrefetchScalarGridSpec(
            num_scalar_prefetch=1,
            grid=(heads // per,),
            in_specs=[own, own, own, side, side]
            + [pl.BlockSpec(grads[0].shape, lambda h, info: (0, 0))] * 2
            + [turned,
                      pl.BlockSpec((per, 1, rows), lambda h, info: (h, 0, 0))]
            + [pl.BlockSpec(memory_space=pl.ANY)] * len(before),
            out_specs=(own, side, side, side),
            scratch_shapes=[pltpu.VMEM((heads * HEAD, rows), BF)],
        ),
        input_output_aliases={10: 0} if again else {},
        compiler_params=pltpu.CompilerParams(vmem_limit_bytes=VMEM_LIMIT),
        cost_estimate=COST,
        name="attend_back",
    )(info, q, k, v, left, right, *grads, attn, total, *before)


JOIN_ROWS = 192


def join_kernel(first, info, own_ref, a_ref, b_ref, *rest):
    dk_ref, dv_ref = rest if first else rest[2:]
    for i, out in enumerate((dk_ref, dv_ref)):
        out[...] = (own_ref[i].astype(F32) + a_ref[i].astype(F32) + b_ref[i].astype(F32)).astype(BF)


def join(part, info, own, a, b, heads, cols, before):
    rows = own.shape[1]
    wide = heads * HEAD
    side = pl.BlockSpec((2, JOIN_ROWS, wide), lambda r, info: (0, r, 0))
    out = pl.BlockSpec((JOIN_ROWS, wide), lambda r, info: (r, info[part] // heads))
    first = before is None
    return pl.pallas_call(
        functools.partial(join_kernel, first),
        out_shape=(jax.ShapeDtypeStruct((rows, cols), BF),) * 2,
        grid_spec=pltpu.PrefetchScalarGridSpec(
            num_scalar_prefetch=1,
            grid=(rows // JOIN_ROWS,),
            in_specs=[side] * 3 + ([] if first else [pl.BlockSpec(memory_space=pl.ANY)] * 2),
            out_specs=(out, out),
        ),
        input_output_aliases={} if first else {4: 0, 5: 1},
        compiler_params=pltpu.CompilerParams(vmem_limit_bytes=VMEM_LIMIT),
        cost_estimate=COST,
        name="join",
    )(info, own, a, b, *(() if first else before))


def hold_kernel(x_ref, *rest):
    del x_ref, rest


def hold(x, *before):
    anywhere = pl.BlockSpec(memory_space=pl.ANY)
    return pl.pallas_call(
        hold_kernel,
        out_shape=jax.ShapeDtypeStruct(x.shape, x.dtype),
        in_specs=[anywhere] * (1 + len(before)),
        out_specs=anywhere,
        input_output_aliases={0: 0},
        cost_estimate=COST,
        name="hold",
    )(x, *before)


def window_kernel(part, info, k_ref, v_ref, *rest):
    out, sems = rest[-2:]
    wide = out.shape[2]
    cols = pl.ds(pl.multiple_of(info[part] * HEAD, wide), wide)
    copies = [
        pltpu.make_async_copy(ref.at[:, cols], out.at[j], sems.at[j])
        for j, ref in enumerate((k_ref, v_ref))
    ]
    for copy in copies:
        copy.start()
    for copy in copies:
        copy.wait()


def window(part, info, k, v, heads, before=()):
    rows = k.shape[0]
    return pl.pallas_call(
        functools.partial(window_kernel, part),
        out_shape=jax.ShapeDtypeStruct((2, rows, heads * HEAD), BF),
        in_specs=[pl.BlockSpec(memory_space=pltpu.SMEM)]
        + [pl.BlockSpec(memory_space=pl.ANY)] * (2 + len(before)),
        out_specs=pl.BlockSpec(memory_space=pltpu.VMEM),
        scratch_shapes=[pltpu.SemaphoreType.DMA((2,))],
        compiler_params=pltpu.CompilerParams(vmem_limit_bytes=VMEM_LIMIT),
        cost_estimate=COST,
        name="window",
    )(info, k, v, *before)


def project_back_kernel(place, *refs):
    pieces, (u_ref, other_ref) = refs[:NZ], refs[NZ:NZ + 2]
    mine_ref, theirs_ref, w = refs[-3:]
    rows = pieces[0].shape[0]
    for i, piece in enumerate(pieces):
        w[pl.ds(pl.multiple_of(place[FROM_Z + i] * rows, rows), rows), :] = piece[...]
    mine_ref[...] = nt(w[...], u_ref[...]).astype(BF)
    theirs_ref[...] = nt(w[...], other_ref[...]).astype(BF)


def project_back(place, pieces, u, other, before=()):
    rows, wide = pieces[0].shape
    tokens = u.shape[0]
    whole = pl.BlockSpec(memory_space=pltpu.VMEM)
    return pl.pallas_call(
        project_back_kernel,
        out_shape=(jax.ShapeDtypeStruct((NZ * rows, tokens), BF),) * 2,
        in_specs=[pl.BlockSpec(memory_space=pltpu.SMEM)] + [whole] * (NZ + 2)
        + [pl.BlockSpec(memory_space=pl.ANY)] * len(before),
        out_specs=(whole, whole),
        scratch_shapes=[pltpu.VMEM((NZ * rows, wide), BF)],
        compiler_params=pltpu.CompilerParams(vmem_limit_bytes=VMEM_LIMIT),
        cost_estimate=COST,
        name="project_back",
    )(place, *pieces, u, other, *before)


def project_kernel(place, *refs):
    turned, pieces = refs[:4], refs[4:4 + 2 * NZ]
    near_ref, far_refs, w = refs[-4], refs[-3:-1], refs[-1]
    rows = pieces[0].shape[0]
    half = NZ * rows
    for i, piece in enumerate(pieces):
        spot = (i // NZ) * half + place[FROM_Z + i % NZ] * rows
        w[pl.ds(pl.multiple_of(spot, rows), rows), :] = piece[...]
    wide = w.shape[1]
    block = wide // 4
    first, second = turned[2][...].T, turned[3][...].T
    for i in range(4):
        cols = slice(i * block, (i + 1) * block)
        there = slice(i % 2 * block, (i % 2 + 1) * block)
        total = nn(first, w[:half, cols]) + nn(second, w[half:, cols])
        far_refs[i // 2][:, there] = total.astype(BF)
    first, second = turned[0][...].T, turned[1][...].T
    for i in range(4):
        cols = slice(i * block, (i + 1) * block)
        near_ref[:, cols] = (nn(first, w[:half, cols]) + nn(second, w[half:, cols])).astype(BF)


def project(place, turned, pieces, before):
    tokens = turned[0].shape[1]
    rows, wide = pieces[0].shape
    whole = pl.BlockSpec(memory_space=pltpu.VMEM)
    return pl.pallas_call(
        project_kernel,
        out_shape=(jax.ShapeDtypeStruct((tokens, wide), BF),)
        + (jax.ShapeDtypeStruct((tokens, wide // 2), BF),) * 2,
        in_specs=[pl.BlockSpec(memory_space=pltpu.SMEM)] + [whole] * (4 + 2 * NZ)
        + [pl.BlockSpec(memory_space=pl.ANY)] * len(before),
        out_specs=(whole,) * 3,
        scratch_shapes=[pltpu.VMEM((2 * NZ * rows, wide), BF)],
        compiler_params=pltpu.CompilerParams(vmem_limit_bytes=VMEM_LIMIT),
        cost_estimate=COST,
        name="project",
    )(place, *turned, *pieces, *before)


def meet_kernel(near_ref, first_ref, second_ref, out_ref):
    half = first_ref.shape[1]
    for i, ref in enumerate((first_ref, second_ref)):
        cols = slice(i * half, (i + 1) * half)
        out_ref[:, cols] = (near_ref[:, cols].astype(F32) + ref[...].astype(F32)).astype(BF)


def meet(near, first, second):
    tokens, wide = near.shape
    block = 128
    spec = pl.BlockSpec((block, wide), lambda i: (i, 0))
    half = pl.BlockSpec((block, wide // 2), lambda i: (i, 0))
    return pl.pallas_call(
        meet_kernel,
        out_shape=jax.ShapeDtypeStruct((tokens, wide), BF),
        grid=(tokens // block,),
        in_specs=[spec, half, half],
        out_specs=spec,
        compiler_params=pltpu.CompilerParams(vmem_limit_bytes=VMEM_LIMIT),
        cost_estimate=COST,
        name="meet",
    )(near, first, second)


def weight_grad_kernel(place, *refs):
    a_refs, u_refs = refs[:4], refs[4:8]
    out_refs, total = refs[-1 - NZ:-1], refs[-1]
    total[...] = sum(nn(a[...], u[...]) for a, u in zip(a_refs, u_refs)).astype(BF)
    rows = out_refs[0].shape[0]
    for i, out in enumerate(out_refs):
        out[...] = total[pl.ds(pl.multiple_of(place[TO_Z + i] * rows, rows), rows), :]


def weight_grad(place, a_list, u_list, before):
    rows, tokens = a_list[0].shape
    wide = u_list[0].shape[1]
    block = wide // WG_STEPS
    sub = rows // NZ
    return pl.pallas_call(
        weight_grad_kernel,
        out_shape=(jax.ShapeDtypeStruct((sub, wide), BF),) * NZ,
        grid_spec=pltpu.PrefetchScalarGridSpec(
            num_scalar_prefetch=1,
            grid=(WG_STEPS,),
            in_specs=[pl.BlockSpec((rows, tokens), lambda i, p: (0, 0))] * 4
            + [pl.BlockSpec((tokens, block), lambda i, p: (0, i))] * 4
            + [pl.BlockSpec(memory_space=pl.ANY)] * len(before),
            out_specs=(pl.BlockSpec((sub, block), lambda i, p: (0, i)),) * NZ,
            scratch_shapes=[pltpu.VMEM((rows, block), BF)],
        ),
        compiler_params=pltpu.CompilerParams(vmem_limit_bytes=VMEM_LIMIT),
        cost_estimate=COST,
        name="weight_grad",
    )(place, *a_list, *u_list, *before)


def sum_columns_kernel(place, *refs):
    pieces, outs = refs[:NZ], refs[-NY:]
    wide = outs[0].shape[1]
    for i, out in enumerate(outs):
        cols = pl.ds(pl.multiple_of(place[TO_Y + i] * wide, wide), wide)
        out[...] = sum(piece[:, cols].astype(F32) for piece in pieces).astype(out.dtype)


def sum_columns(place, pieces, before):
    rows, cols = pieces[0].shape
    whole = pl.BlockSpec(memory_space=pltpu.VMEM)
    return pl.pallas_call(
        sum_columns_kernel,
        out_shape=tuple(
            jax.ShapeDtypeStruct((rows, cols // NY), F32 if i == 0 else BF) for i in range(NY)
        ),
        in_specs=[pl.BlockSpec(memory_space=pltpu.SMEM)] + [whole] * NZ
        + [pl.BlockSpec(memory_space=pl.ANY)] * len(before),
        out_specs=(whole,) * NY,
        compiler_params=pltpu.CompilerParams(vmem_limit_bytes=VMEM_LIMIT),
        cost_estimate=COST,
        name="sum_columns",
    )(place, *pieces, *before)


def place_kernel(spots, *refs):
    out_ref = refs[-1]
    wide = refs[0].shape[1]
    for j, ref in enumerate(refs[:NY]):
        out_ref[:, pl.ds(pl.multiple_of(spots[FROM_Y + j] * wide, wide), wide)] = ref[...].astype(F32)


def place_columns(spots, pieces, before):
    rows, cols = pieces[0].shape
    whole = pl.BlockSpec(memory_space=pltpu.VMEM)
    return pl.pallas_call(
        place_kernel,
        out_shape=jax.ShapeDtypeStruct((rows, len(pieces) * cols), F32),
        in_specs=[pl.BlockSpec(memory_space=pltpu.SMEM)] + [whole] * NY
        + [pl.BlockSpec(memory_space=pl.ANY)] * len(before),
        out_specs=whole,
        cost_estimate=COST,
        name="place_columns",
    )(spots, *pieces, *before)


def add(*terms):
    return functools.reduce(lambda s, t: s + t.astype(F32), terms[1:], terms[0].astype(F32))


def on_device(query, key_in, value_in, out_weight, grad_out, neighbours):
    q, k, v, upstream = query[0], key_in[0], value_in[0], grad_out[0]
    rows, cols = q.shape
    half = cols // 2
    heads = half // HEAD
    dp = lax.axis_index("dp")
    tile = lax.axis_index("space")
    a, z, c = dp // (NZ * NC), (dp // NC) % NZ, dp % NC
    lo, y = tile // NY, tile % NY

    info = [a * heads, (1 - a) * heads, tile, c]
    info += [(z + i) % NZ for i in (0, 3, 1, 2)] + [(z + i) % NZ for i in range(NZ)]
    info += [(y + i) % NY for i in range(NY)] + [(y + i) % NY for i in (0, 3, 1, 2)]
    info = jnp.concatenate([jnp.stack(info).astype(jnp.int32), neighbours.reshape(-1)])
    pair = window(0, info, k, v, heads)
    near0 = (to_next(pair), to_previous(pair))
    up_core = move_core(upstream)

    def around(x):
        up, down = move_z(x, 1), move_z(x, 3)
        return [x, up, down]

    w0 = around(out_weight)
    w0[1] = hold(w0[1], up_core)
    later = window(1, info, k, v, heads, w0[1:2])
    pair = hold(later, *near0, *w0[1:])
    near1 = (to_next(pair), to_previous(pair))

    cross = move_cross(out_weight)
    w0.append(move_z(w0[1], 1))

    up_cross = move_cross(hold(upstream, cross))

    def back(w, before):
        mine, theirs = project_back(info, w, upstream, up_core, before)
        return mine, move_core(theirs)

    attn0, total0 = attend(0, info, q, k, v, *near0, heads)
    grad0 = back(w0, (attn0,))
    w1 = around(hold(cross, pair))
    attn1, total1 = attend(1, info, q, k, v, *near1, heads, (grad0[0], w1[1], w1[2]))
    w1.append(move_z(w1[0], 2))
    up_cross = hold(up_cross, attn1)
    dq, own0, to_left, to_right = attend_back(
        0, info, q, k, v, *near0, grad0, attn0, total0, heads, (attn1,), False
    )
    sent0 = (to_next(to_right), to_previous(to_left))

    def pick(attn, core):
        parts = attn.reshape(NZ, NC, -1, rows)
        sub = parts.shape[2]
        return lax.dynamic_slice(parts, (0, core, 0, 0), (NZ, 1, sub, rows)).reshape(
            NZ * sub, rows
        )

    own_part, core_part = pick(attn1, c), pick(attn1, 1 - c)
    a_list = [
        pick(attn0, c),
        move_core(pick(attn0, 1 - c)),
        move_cross(own_part),
        move_cross_core(core_part),
    ]
    grad1 = back(w1, (own0,))
    core_far = move_core(core_part)
    dq, own1, to_left, to_right = attend_back(
        1, info, q, k, v, *near1, grad1, attn1, total1, heads, (dq, core_far), True
    )
    sent1 = (to_next(to_right), to_previous(to_left))
    u_list = [upstream, up_core, up_cross, move_core(up_cross)]
    pieces = weight_grad(info, a_list, u_list, (own1,) + sent0)
    turned = [a_list[0], own_part, a_list[1], core_far]
    near, *far = project(info, turned, w0 + w1, pieces[:1])
    mixed = meet(near, *[move_core(t) for t in far])
    done = join(0, info, own0, *sent0, heads, cols, None)
    done = join(1, info, own1, *sent1, heads, cols, done)

    columns = sum_columns(info, (pieces[0],) + tuple(move_z(pieces[i], i) for i in (1, 3, 2)), done)
    mine = add(columns[0], *[move_y(columns[i], i) for i in (1, 3, 2)]).astype(BF)
    mine = add(mine, move_lo(mine)).astype(BF)
    gathered = [mine] + [move_y(mine, i) for i in (1, 3, 2)]
    grad_weight = place_columns(info, gathered, (mixed,))
    dk, dv = done
    return (mixed[None], dq[None], dk[None], dv[None], grad_weight)


def solution(mesh):
    return jax.shard_map(
        on_device,
        mesh=mesh,
        in_specs=(
            P("dp", "space", None),
            P("dp", "space", None),
            P("dp", "space", None),
            P("dp", None),
            P("dp", "space", None),
            P(),
        ),
        out_specs=(
            P("dp", "space", None),
            P("dp", "space", None),
            P("dp", "space", None),
            P("dp", "space", None),
            P("dp", None),
        ),
        check_vma=False,
    )
```

```python
import functools
import math

import jax
import jax.numpy as jnp
from jax import lax
from jax.experimental import pallas as pl
from jax.experimental.pallas import tpu as pltpu
from jax.sharding import PartitionSpec as P

HEAD = 128
SCALE = 1.0 / math.sqrt(HEAD)
LOG2_SCALE = SCALE * math.log2(math.e)
FAR = 1e30
TILE_AT, CORE_AT, FROM_Z, TO_Z, TO_Y, FROM_Y, AROUND = 2, 3, 4, 8, 12, 16, 20
SLOTS = 3
COST = pl.CostEstimate(flops=1000, bytes_accessed=1000, transcendentals=0)
BF = jnp.bfloat16
F32 = jnp.float32
VMEM_LIMIT = 60 * 1024 * 1024
WG_STEPS = 3

NX, NZ, NC, NL, NY = 2, 4, 2, 2, 4
NS = NL * NY


def moves(change):
    pairs = []
    for a in range(NX):
        for z in range(NZ):
            for c in range(NC):
                for l in range(NL):
                    for y in range(NY):
                        b, w, d, m, v = change(a, z, c, l, y)
                        src = ((a * NZ + z) * NC + c) * NS + l * NY + y
                        dst = ((b * NZ + w) * NC + d) * NS + m * NY + v
                        pairs.append((src, dst))
    return pairs


def move(x, change):
    return lax.ppermute(x, ("dp", "space"), moves(change))


def move_core(x):
    return move(x, lambda a, z, c, l, y: (a, z, 1 - c, l, y))


def move_lo(x):
    return move(x, lambda a, z, c, l, y: (a, z, c, 1 - l, y))


def move_lo_core(x):
    return move(x, lambda a, z, c, l, y: (a, z, 1 - c, 1 - l, y))


def move_hi(x):
    return move(x, lambda a, z, c, l, y: (1 - a, z, c, l, y))


def move_cross(x):
    return move(x, lambda a, z, c, l, y: (1 - a, z, c, 1 - l, y))


def move_cross_core(x):
    return move(x, lambda a, z, c, l, y: (1 - a, z, 1 - c, 1 - l, y))


def move_z(x, k):
    return move(x, lambda a, z, c, l, y: (a, (z + k) % NZ, c, l, y))


def move_y(x, k):
    return move(x, lambda a, z, c, l, y: (a, z, c, l, (y + k) % NY))


def to_next(x):
    return lax.ppermute(x, "space", [(i, i + 1) for i in range(NS - 1)])


def to_previous(x):
    return lax.ppermute(x, "space", [(i + 1, i) for i in range(NS - 1)])


def nt(a, b):
    return lax.dot_general(a, b, (((1,), (1,)), ((), ())), preferred_element_type=F32)


def tn(a, b):
    return lax.dot_general(a, b, (((0,), (0,)), ((), ())), preferred_element_type=F32)


def nn(a, b):
    return lax.dot_general(a, b, (((1,), (0,)), ((), ())), preferred_element_type=F32)


PER_F = 2
PER_B = 2


def windows(live, shift):
    factors = [jnp.where(on, LOG2_SCALE, 0.0) for on in live]
    return factors, [jnp.where(on, shift, FAR) for on in live]


def forward_head(live, cols, q_ref, k_ref, v_ref, left_ref, right_ref):
    q = q_ref[:, cols]
    keys = (left_ref[0, :, cols], k_ref[:, cols], right_ref[0, :, cols])
    values = (left_ref[1, :, cols], v_ref[:, cols], right_ref[1, :, cols])
    scores = [nt(k, q) for k in keys]
    tops = [jnp.max(s, axis=0, keepdims=True) for s in scores]
    top = tops[1]
    for j in (0, 2):
        top = jnp.maximum(top, jnp.where(live[j // 2], tops[j], -FAR))
    top = top * LOG2_SCALE
    total = jnp.zeros_like(top)
    acc = jnp.zeros((HEAD, q.shape[0]), F32)
    for j in range(3):
        factor = LOG2_SCALE if j == 1 else jnp.where(live[j // 2], LOG2_SCALE, 0.0)
        shift = top if j == 1 else jnp.where(live[j // 2], top, FAR)
        p = jnp.exp2(scores[j] * factor - shift)
        total = total + jnp.sum(p, axis=0, keepdims=True)
        acc = acc + tn(values[j], p.astype(BF))
    return (acc / total).astype(BF), top + jnp.log2(total)


def live_sides(info):
    tile = info[TILE_AT]
    found = [jnp.zeros((), jnp.bool_)] * 2
    for i in range(SLOTS):
        entry = info[AROUND + SLOTS * tile + i]
        found = [on | ((entry == tile + d) & (entry >= 0)) for on, d in zip(found, (-1, 1))]
    return found


def forward_kernel(per, part, info, q_ref, k_ref, v_ref, left_ref, right_ref, *rest):
    attn_ref, total_ref = rest[-2:]
    live = live_sides(info)
    for i in range(per):
        cols = slice(i * HEAD, (i + 1) * HEAD)
        attn_ref[cols, :], total_ref[i] = forward_head(
            live, cols, q_ref, k_ref, v_ref, left_ref, right_ref
        )


def attend(part, info, q, k, v, left, right, heads, before=()):
    rows = q.shape[0]
    per = PER_F
    own = pl.BlockSpec((rows, per * HEAD), lambda h, info: (0, info[part] // per + h))
    side = pl.BlockSpec((2, rows, per * HEAD), lambda h, info: (0, 0, h))
    return pl.pallas_call(
        functools.partial(forward_kernel, per, part),
        out_shape=(
            jax.ShapeDtypeStruct((heads * HEAD, rows), BF),
            jax.ShapeDtypeStruct((heads, 1, rows), F32),
        ),
        grid_spec=pltpu.PrefetchScalarGridSpec(
            num_scalar_prefetch=1,
            grid=(heads // per,),
            in_specs=[own, own, own, side, side] + [pl.BlockSpec(memory_space=pl.ANY)] * len(before),
            out_specs=(
                pl.BlockSpec((per * HEAD, rows), lambda h, info: (h, 0)),
                pl.BlockSpec((per, 1, rows), lambda h, info: (h, 0, 0)),
            ),
        ),
        compiler_params=pltpu.CompilerParams(vmem_limit_bytes=VMEM_LIMIT),
        cost_estimate=COST,
        name="attend",
    )(info, q, k, v, left, right, *before)


def backward_kernel(per, part, info, q_ref, k_ref, v_ref, left_ref, right_ref, mine_ref, theirs_ref, attn_ref, total_ref, *rest):
    dq_ref, own_ref, to_left_ref, to_right_ref, grad_ref = rest[-5:]
    step = pl.program_id(0)

    @pl.when(step == 0)
    def _():
        size = mine_ref.shape[0] // NZ
        for i in range(NZ):
            for ref, core in ((mine_ref, info[CORE_AT]), (theirs_ref, 1 - info[CORE_AT])):
                spot = pl.multiple_of((NC * i + core) * size, size)
                grad_ref[pl.ds(spot, size), :] = ref[i * size:(i + 1) * size, :]

    outs = (to_left_ref, own_ref, to_right_ref)
    live = live_sides(info)
    for i in range(per):
        cols = slice(i * HEAD, (i + 1) * HEAD)
        q = q_ref[:, cols]
        here = pl.multiple_of((step * per + i) * HEAD, HEAD)
        g = grad_ref[pl.ds(here, HEAD), :]
        total = total_ref[i]
        delta = jnp.sum(g.astype(F32) * attn_ref[cols, :].astype(F32), axis=0, keepdims=True)
        keys = (left_ref[0, :, cols], k_ref[:, cols], right_ref[0, :, cols])
        values = (left_ref[1, :, cols], v_ref[:, cols], right_ref[1, :, cols])
        dq = jnp.zeros((HEAD, q.shape[0]), F32)
        for j in range(3):
            k, v = keys[j], values[j]
            factor = LOG2_SCALE if j == 1 else jnp.where(live[j // 2], LOG2_SCALE, 0.0)
            shift = total if j == 1 else jnp.where(live[j // 2], total, FAR)
            w = jnp.exp2(nt(k, q) * factor - shift)
            outs[j][1, :, cols] = nt(w.astype(BF), g).astype(BF)
            ds = (w * (nn(v, g) - delta)).astype(BF)
            outs[j][0, :, cols] = (nn(ds, q) * SCALE).astype(BF)
            dq = dq + tn(k, ds)
        dq_ref[:, cols] = (dq * SCALE).T.astype(BF)


def attend_back(part, info, q, k, v, left, right, grads, attn, total, heads, before, again):
    rows, cols = q.shape
    per = PER_B
    own = pl.BlockSpec((rows, per * HEAD), lambda h, info: (0, info[part] // per + h))
    side = pl.BlockSpec((2, rows, per * HEAD), lambda h, info: (0, 0, h))
    turned = pl.BlockSpec((per * HEAD, rows), lambda h, info: (h, 0))
    return pl.pallas_call(
        functools.partial(backward_kernel, per, part),
        out_shape=(jax.ShapeDtypeStruct((rows, cols), BF),)
        + (jax.ShapeDtypeStruct((2, rows, heads * HEAD), BF),) * 3,
        grid_spec=pltpu.PrefetchScalarGridSpec(
            num_scalar_prefetch=1,
            grid=(heads // per,),
            in_specs=[own, own, own, side, side]
            + [pl.BlockSpec(grads[0].shape, lambda h, info: (0, 0))] * 2
            + [turned,
                      pl.BlockSpec((per, 1, rows), lambda h, info: (h, 0, 0))]
            + [pl.BlockSpec(memory_space=pl.ANY)] * len(before),
            out_specs=(own, side, side, side),
            scratch_shapes=[pltpu.VMEM((heads * HEAD, rows), BF)],
        ),
        input_output_aliases={10: 0} if again else {},
        compiler_params=pltpu.CompilerParams(vmem_limit_bytes=VMEM_LIMIT),
        cost_estimate=COST,
        name="attend_back",
    )(info, q, k, v, left, right, *grads, attn, total, *before)


JOIN_ROWS = 192


def join_kernel(first, info, own_ref, a_ref, b_ref, *rest):
    dk_ref, dv_ref = rest if first else rest[2:]
    for i, out in enumerate((dk_ref, dv_ref)):
        out[...] = (own_ref[i].astype(F32) + a_ref[i].astype(F32) + b_ref[i].astype(F32)).astype(BF)


def join(part, info, own, a, b, heads, cols, before):
    rows = own.shape[1]
    wide = heads * HEAD
    side = pl.BlockSpec((2, JOIN_ROWS, wide), lambda r, info: (0, r, 0))
    out = pl.BlockSpec((JOIN_ROWS, wide), lambda r, info: (r, info[part] // heads))
    first = before is None
    return pl.pallas_call(
        functools.partial(join_kernel, first),
        out_shape=(jax.ShapeDtypeStruct((rows, cols), BF),) * 2,
        grid_spec=pltpu.PrefetchScalarGridSpec(
            num_scalar_prefetch=1,
            grid=(rows // JOIN_ROWS,),
            in_specs=[side] * 3 + ([] if first else [pl.BlockSpec(memory_space=pl.ANY)] * 2),
            out_specs=(out, out),
        ),
        input_output_aliases={} if first else {4: 0, 5: 1},
        compiler_params=pltpu.CompilerParams(vmem_limit_bytes=VMEM_LIMIT),
        cost_estimate=COST,
        name="join",
    )(info, own, a, b, *(() if first else before))


def hold_kernel(x_ref, *rest):
    del x_ref, rest


def hold(x, *before):
    anywhere = pl.BlockSpec(memory_space=pl.ANY)
    return pl.pallas_call(
        hold_kernel,
        out_shape=jax.ShapeDtypeStruct(x.shape, x.dtype),
        in_specs=[anywhere] * (1 + len(before)),
        out_specs=anywhere,
        input_output_aliases={0: 0},
        cost_estimate=COST,
        name="hold",
    )(x, *before)


def window_kernel(part, info, k_ref, v_ref, *rest):
    out, sems = rest[-2:]
    wide = out.shape[2]
    cols = pl.ds(pl.multiple_of(info[part] * HEAD, wide), wide)
    copies = [
        pltpu.make_async_copy(ref.at[:, cols], out.at[j], sems.at[j])
        for j, ref in enumerate((k_ref, v_ref))
    ]
    for copy in copies:
        copy.start()
    for copy in copies:
        copy.wait()


def window(part, info, k, v, heads, before=()):
    rows = k.shape[0]
    return pl.pallas_call(
        functools.partial(window_kernel, part),
        out_shape=jax.ShapeDtypeStruct((2, rows, heads * HEAD), BF),
        in_specs=[pl.BlockSpec(memory_space=pltpu.SMEM)]
        + [pl.BlockSpec(memory_space=pl.ANY)] * (2 + len(before)),
        out_specs=pl.BlockSpec(memory_space=pltpu.VMEM),
        scratch_shapes=[pltpu.SemaphoreType.DMA((2,))],
        compiler_params=pltpu.CompilerParams(vmem_limit_bytes=VMEM_LIMIT),
        cost_estimate=COST,
        name="window",
    )(info, k, v, *before)


def project_back_kernel(place, *refs):
    pieces, (u_ref, other_ref) = refs[:NZ], refs[NZ:NZ + 2]
    mine_ref, theirs_ref, w = refs[-3:]
    rows = pieces[0].shape[0]
    for i, piece in enumerate(pieces):
        w[pl.ds(pl.multiple_of(place[FROM_Z + i] * rows, rows), rows), :] = piece[...]
    mine_ref[...] = nt(w[...], u_ref[...]).astype(BF)
    theirs_ref[...] = nt(w[...], other_ref[...]).astype(BF)


def project_back(place, pieces, u, other, before=()):
    rows, wide = pieces[0].shape
    tokens = u.shape[0]
    whole = pl.BlockSpec(memory_space=pltpu.VMEM)
    return pl.pallas_call(
        project_back_kernel,
        out_shape=(jax.ShapeDtypeStruct((NZ * rows, tokens), BF),) * 2,
        in_specs=[pl.BlockSpec(memory_space=pltpu.SMEM)] + [whole] * (NZ + 2)
        + [pl.BlockSpec(memory_space=pl.ANY)] * len(before),
        out_specs=(whole, whole),
        scratch_shapes=[pltpu.VMEM((NZ * rows, wide), BF)],
        compiler_params=pltpu.CompilerParams(vmem_limit_bytes=VMEM_LIMIT),
        cost_estimate=COST,
        name="project_back",
    )(place, *pieces, u, other, *before)


def project_kernel(place, *refs):
    turned, pieces = refs[:4], refs[4:4 + 2 * NZ]
    near_ref, far_refs, w = refs[-4], refs[-3:-1], refs[-1]
    rows = pieces[0].shape[0]
    half = NZ * rows
    for i, piece in enumerate(pieces):
        spot = (i // NZ) * half + place[FROM_Z + i % NZ] * rows
        w[pl.ds(pl.multiple_of(spot, rows), rows), :] = piece[...]
    wide = w.shape[1]
    block = wide // 4
    first, second = turned[2][...].T, turned[3][...].T
    for i in range(4):
        cols = slice(i * block, (i + 1) * block)
        there = slice(i % 2 * block, (i % 2 + 1) * block)
        total = nn(first, w[:half, cols]) + nn(second, w[half:, cols])
        far_refs[i // 2][:, there] = total.astype(BF)
    first, second = turned[0][...].T, turned[1][...].T
    for i in range(4):
        cols = slice(i * block, (i + 1) * block)
        near_ref[:, cols] = (nn(first, w[:half, cols]) + nn(second, w[half:, cols])).astype(BF)


def project(place, turned, pieces, before):
    tokens = turned[0].shape[1]
    rows, wide = pieces[0].shape
    whole = pl.BlockSpec(memory_space=pltpu.VMEM)
    return pl.pallas_call(
        project_kernel,
        out_shape=(jax.ShapeDtypeStruct((tokens, wide), BF),)
        + (jax.ShapeDtypeStruct((tokens, wide // 2), BF),) * 2,
        in_specs=[pl.BlockSpec(memory_space=pltpu.SMEM)] + [whole] * (4 + 2 * NZ)
        + [pl.BlockSpec(memory_space=pl.ANY)] * len(before),
        out_specs=(whole,) * 3,
        scratch_shapes=[pltpu.VMEM((2 * NZ * rows, wide), BF)],
        compiler_params=pltpu.CompilerParams(vmem_limit_bytes=VMEM_LIMIT),
        cost_estimate=COST,
        name="project",
    )(place, *turned, *pieces, *before)


def meet_kernel(near_ref, first_ref, second_ref, out_ref):
    half = first_ref.shape[1]
    for i, ref in enumerate((first_ref, second_ref)):
        cols = slice(i * half, (i + 1) * half)
        out_ref[:, cols] = (near_ref[:, cols].astype(F32) + ref[...].astype(F32)).astype(BF)


def meet(near, first, second):
    tokens, wide = near.shape
    block = 128
    spec = pl.BlockSpec((block, wide), lambda i: (i, 0))
    half = pl.BlockSpec((block, wide // 2), lambda i: (i, 0))
    return pl.pallas_call(
        meet_kernel,
        out_shape=jax.ShapeDtypeStruct((tokens, wide), BF),
        grid=(tokens // block,),
        in_specs=[spec, half, half],
        out_specs=spec,
        compiler_params=pltpu.CompilerParams(vmem_limit_bytes=VMEM_LIMIT),
        cost_estimate=COST,
        name="meet",
    )(near, first, second)


def weight_grad_kernel(place, *refs):
    a_refs, u_refs = refs[:4], refs[4:8]
    out_refs, total = refs[-1 - NZ:-1], refs[-1]
    left = jnp.concatenate([a[...] for a in a_refs], axis=1)
    right = jnp.concatenate([u[...] for u in u_refs], axis=0)
    total[...] = nn(left, right).astype(BF)
    rows = out_refs[0].shape[0]
    for i, out in enumerate(out_refs):
        out[...] = total[pl.ds(pl.multiple_of(place[TO_Z + i] * rows, rows), rows), :]


def weight_grad(place, a_list, u_list, before):
    rows, tokens = a_list[0].shape
    wide = u_list[0].shape[1]
    block = wide // WG_STEPS
    sub = rows // NZ
    return pl.pallas_call(
        weight_grad_kernel,
        out_shape=(jax.ShapeDtypeStruct((sub, wide), BF),) * NZ,
        grid_spec=pltpu.PrefetchScalarGridSpec(
            num_scalar_prefetch=1,
            grid=(WG_STEPS,),
            in_specs=[pl.BlockSpec((rows, tokens), lambda i, p: (0, 0))] * 4
            + [pl.BlockSpec((tokens, block), lambda i, p: (0, i))] * 4
            + [pl.BlockSpec(memory_space=pl.ANY)] * len(before),
            out_specs=(pl.BlockSpec((sub, block), lambda i, p: (0, i)),) * NZ,
            scratch_shapes=[pltpu.VMEM((rows, block), BF)],
        ),
        compiler_params=pltpu.CompilerParams(vmem_limit_bytes=VMEM_LIMIT),
        cost_estimate=COST,
        name="weight_grad",
    )(place, *a_list, *u_list, *before)


def sum_columns_kernel(place, *refs):
    pieces, outs = refs[:NZ], refs[-NY:]
    wide = outs[0].shape[1]
    for i, out in enumerate(outs):
        cols = pl.ds(pl.multiple_of(place[TO_Y + i] * wide, wide), wide)
        out[...] = sum(piece[:, cols].astype(F32) for piece in pieces).astype(out.dtype)


def sum_columns(place, pieces, before):
    rows, cols = pieces[0].shape
    whole = pl.BlockSpec(memory_space=pltpu.VMEM)
    return pl.pallas_call(
        sum_columns_kernel,
        out_shape=tuple(
            jax.ShapeDtypeStruct((rows, cols // NY), F32 if i == 0 else BF) for i in range(NY)
        ),
        in_specs=[pl.BlockSpec(memory_space=pltpu.SMEM)] + [whole] * NZ
        + [pl.BlockSpec(memory_space=pl.ANY)] * len(before),
        out_specs=(whole,) * NY,
        compiler_params=pltpu.CompilerParams(vmem_limit_bytes=VMEM_LIMIT),
        cost_estimate=COST,
        name="sum_columns",
    )(place, *pieces, *before)


def place_kernel(spots, *refs):
    out_ref = refs[-1]
    wide = refs[0].shape[1]
    for j, ref in enumerate(refs[:NY]):
        out_ref[:, pl.ds(pl.multiple_of(spots[FROM_Y + j] * wide, wide), wide)] = ref[...].astype(F32)


def place_columns(spots, pieces, before):
    rows, cols = pieces[0].shape
    whole = pl.BlockSpec(memory_space=pltpu.VMEM)
    return pl.pallas_call(
        place_kernel,
        out_shape=jax.ShapeDtypeStruct((rows, len(pieces) * cols), F32),
        in_specs=[pl.BlockSpec(memory_space=pltpu.SMEM)] + [whole] * NY
        + [pl.BlockSpec(memory_space=pl.ANY)] * len(before),
        out_specs=whole,
        cost_estimate=COST,
        name="place_columns",
    )(spots, *pieces, *before)


def add(*terms):
    return functools.reduce(lambda s, t: s + t.astype(F32), terms[1:], terms[0].astype(F32))


def on_device(query, key_in, value_in, out_weight, grad_out, neighbours):
    q, k, v, upstream = query[0], key_in[0], value_in[0], grad_out[0]
    rows, cols = q.shape
    half = cols // 2
    heads = half // HEAD
    dp = lax.axis_index("dp")
    tile = lax.axis_index("space")
    a, z, c = dp // (NZ * NC), (dp // NC) % NZ, dp % NC
    lo, y = tile // NY, tile % NY

    info = [a * heads, (1 - a) * heads, tile, c]
    info += [(z + i) % NZ for i in (0, 3, 1, 2)] + [(z + i) % NZ for i in range(NZ)]
    info += [(y + i) % NY for i in range(NY)] + [(y + i) % NY for i in (0, 3, 1, 2)]
    info = jnp.concatenate([jnp.stack(info).astype(jnp.int32), neighbours.reshape(-1)])
    pair = window(0, info, k, v, heads)
    near0 = (to_next(pair), to_previous(pair))
    up_core = move_core(upstream)

    def around(x):
        up, down = move_z(x, 1), move_z(x, 3)
        return [x, up, down]

    w0 = around(out_weight)
    w0[1] = hold(w0[1], up_core)
    later = window(1, info, k, v, heads, w0[1:2])
    pair = hold(later, *near0, *w0[1:])
    near1 = (to_next(pair), to_previous(pair))

    cross = move_cross(out_weight)
    w0.append(move_z(w0[1], 1))

    up_cross = move_cross(hold(upstream, cross))

    def back(w, before):
        mine, theirs = project_back(info, w, upstream, up_core, before)
        return mine, move_core(theirs)

    attn0, total0 = attend(0, info, q, k, v, *near0, heads)
    grad0 = back(w0, (attn0,))
    w1 = around(hold(cross, pair))
    dq, own0, to_left, to_right = attend_back(
        0, info, q, k, v, *near0, grad0, attn0, total0, heads, (w1[1], w1[2]), False
    )
    w1.append(move_z(hold(w1[0], grad0[0]), 2))
    attn1, total1 = attend(1, info, q, k, v, *near1, heads, (own0, w1[3]))
    up_cross = hold(up_cross, attn1)
    sent0 = (to_next(to_right), to_previous(to_left))

    def pick(attn, core):
        parts = attn.reshape(NZ, NC, -1, rows)
        sub = parts.shape[2]
        return lax.dynamic_slice(parts, (0, core, 0, 0), (NZ, 1, sub, rows)).reshape(
            NZ * sub, rows
        )

    own_part, core_part = pick(attn1, c), pick(attn1, 1 - c)
    a_list = [
        pick(attn0, c),
        move_core(pick(attn0, 1 - c)),
        move_cross(own_part),
        move_cross_core(core_part),
    ]
    grad1 = back(w1, (attn1,))
    core_far = move_core(core_part)
    dq, own1, to_left, to_right = attend_back(
        1, info, q, k, v, *near1, grad1, attn1, total1, heads, (dq, core_far), True
    )
    sent1 = (to_next(to_right), to_previous(to_left))
    u_list = [upstream, up_core, up_cross, move_core(up_cross)]
    pieces = weight_grad(info, a_list, u_list, (own1,))
    turned = [a_list[0], own_part, a_list[1], core_far]
    near, *far = project(info, turned, w0 + w1, pieces[:1] + sent0)
    mixed = meet(near, *[move_core(t) for t in far])
    done = join(0, info, own0, *sent0, heads, cols, None)
    done = join(1, info, own1, *sent1, heads, cols, done)

    columns = sum_columns(info, (pieces[0],) + tuple(move_z(pieces[i], i) for i in (1, 3, 2)), done)
    mine = add(columns[0], *[move_y(columns[i], i) for i in (1, 3, 2)]).astype(BF)
    mine = add(mine, move_lo(mine)).astype(BF)
    gathered = [mine] + [move_y(mine, i) for i in (1, 3, 2)]
    grad_weight = place_columns(info, gathered, (mixed,))
    dk, dv = done
    return (mixed[None], dq[None], dk[None], dv[None], grad_weight)


def solution(mesh):
    return jax.shard_map(
        on_device,
        mesh=mesh,
        in_specs=(
            P("dp", "space", None),
            P("dp", "space", None),
            P("dp", "space", None),
            P("dp", None),
            P("dp", "space", None),
            P(),
        ),
        out_specs=(
            P("dp", "space", None),
            P("dp", "space", None),
            P("dp", "space", None),
            P("dp", "space", None),
            P("dp", None),
        ),
        check_vma=False,
    )
```

```python
import functools
import math

import jax
import jax.numpy as jnp
from jax import lax
from jax.experimental import pallas as pl
from jax.experimental.pallas import tpu as pltpu
from jax.sharding import PartitionSpec as P

HEAD = 128
SCALE = 1.0 / math.sqrt(HEAD)
LOG2_SCALE = SCALE * math.log2(math.e)
FAR = 1e30
TILE_AT, CORE_AT, FROM_Z, TO_Z, TO_Y, FROM_Y, AROUND = 2, 3, 4, 8, 12, 16, 20
SLOTS = 3
COST = pl.CostEstimate(flops=1000, bytes_accessed=1000, transcendentals=0)
BF = jnp.bfloat16
F32 = jnp.float32
VMEM_LIMIT = 60 * 1024 * 1024
WG_STEPS = 3

NX, NZ, NC, NL, NY = 2, 4, 2, 2, 4
NS = NL * NY


def moves(change):
    pairs = []
    for a in range(NX):
        for z in range(NZ):
            for c in range(NC):
                for l in range(NL):
                    for y in range(NY):
                        b, w, d, m, v = change(a, z, c, l, y)
                        src = ((a * NZ + z) * NC + c) * NS + l * NY + y
                        dst = ((b * NZ + w) * NC + d) * NS + m * NY + v
                        pairs.append((src, dst))
    return pairs


def move(x, change):
    return lax.ppermute(x, ("dp", "space"), moves(change))


def move_core(x):
    return move(x, lambda a, z, c, l, y: (a, z, 1 - c, l, y))


def move_lo(x):
    return move(x, lambda a, z, c, l, y: (a, z, c, 1 - l, y))


def move_lo_core(x):
    return move(x, lambda a, z, c, l, y: (a, z, 1 - c, 1 - l, y))


def move_hi(x):
    return move(x, lambda a, z, c, l, y: (1 - a, z, c, l, y))


def move_cross(x):
    return move(x, lambda a, z, c, l, y: (1 - a, z, c, 1 - l, y))


def move_cross_core(x):
    return move(x, lambda a, z, c, l, y: (1 - a, z, 1 - c, 1 - l, y))


def move_z(x, k):
    return move(x, lambda a, z, c, l, y: (a, (z + k) % NZ, c, l, y))


def move_y(x, k):
    return move(x, lambda a, z, c, l, y: (a, z, c, l, (y + k) % NY))


def to_next(x):
    return lax.ppermute(x, "space", [(i, i + 1) for i in range(NS - 1)])


def to_previous(x):
    return lax.ppermute(x, "space", [(i + 1, i) for i in range(NS - 1)])


def nt(a, b):
    return lax.dot_general(a, b, (((1,), (1,)), ((), ())), preferred_element_type=F32)


def tn(a, b):
    return lax.dot_general(a, b, (((0,), (0,)), ((), ())), preferred_element_type=F32)


def nn(a, b):
    return lax.dot_general(a, b, (((1,), (0,)), ((), ())), preferred_element_type=F32)


PER_F = 2
PER_B = 2


def windows(live, shift):
    factors = [jnp.where(on, LOG2_SCALE, 0.0) for on in live]
    return factors, [jnp.where(on, shift, FAR) for on in live]


def forward_head(live, cols, q_ref, k_ref, v_ref, left_ref, right_ref):
    q = q_ref[:, cols]
    keys = (left_ref[0, :, cols], k_ref[:, cols], right_ref[0, :, cols])
    values = (left_ref[1, :, cols], v_ref[:, cols], right_ref[1, :, cols])
    scores = [nt(k, q) for k in keys]
    tops = [jnp.max(s, axis=0, keepdims=True) for s in scores]
    top = tops[1]
    for j in (0, 2):
        top = jnp.maximum(top, jnp.where(live[j // 2], tops[j], -FAR))
    top = top * LOG2_SCALE
    total = jnp.zeros_like(top)
    acc = jnp.zeros((HEAD, q.shape[0]), F32)
    for j in range(3):
        factor = LOG2_SCALE if j == 1 else jnp.where(live[j // 2], LOG2_SCALE, 0.0)
        shift = top if j == 1 else jnp.where(live[j // 2], top, FAR)
        p = jnp.exp2(scores[j] * factor - shift)
        total = total + jnp.sum(p, axis=0, keepdims=True)
        acc = acc + tn(values[j], p.astype(BF))
    return (acc / total).astype(BF), top + jnp.log2(total)


def live_sides(info):
    tile = info[TILE_AT]
    found = [jnp.zeros((), jnp.bool_)] * 2
    for i in range(SLOTS):
        entry = info[AROUND + SLOTS * tile + i]
        found = [on | ((entry == tile + d) & (entry >= 0)) for on, d in zip(found, (-1, 1))]
    return found


def forward_kernel(per, part, info, q_ref, k_ref, v_ref, left_ref, right_ref, *rest):
    attn_ref, total_ref = rest[-2:]
    live = live_sides(info)
    for i in range(per):
        cols = slice(i * HEAD, (i + 1) * HEAD)
        attn_ref[cols, :], total_ref[i] = forward_head(
            live, cols, q_ref, k_ref, v_ref, left_ref, right_ref
        )


def attend(part, info, q, k, v, left, right, heads, before=()):
    rows = q.shape[0]
    per = PER_F
    own = pl.BlockSpec((rows, per * HEAD), lambda h, info: (0, info[part] // per + h))
    side = pl.BlockSpec((2, rows, per * HEAD), lambda h, info: (0, 0, h))
    return pl.pallas_call(
        functools.partial(forward_kernel, per, part),
        out_shape=(
            jax.ShapeDtypeStruct((heads * HEAD, rows), BF),
            jax.ShapeDtypeStruct((heads, 1, rows), F32),
        ),
        grid_spec=pltpu.PrefetchScalarGridSpec(
            num_scalar_prefetch=1,
            grid=(heads // per,),
            in_specs=[own, own, own, side, side] + [pl.BlockSpec(memory_space=pl.ANY)] * len(before),
            out_specs=(
                pl.BlockSpec((per * HEAD, rows), lambda h, info: (h, 0)),
                pl.BlockSpec((per, 1, rows), lambda h, info: (h, 0, 0)),
            ),
        ),
        compiler_params=pltpu.CompilerParams(vmem_limit_bytes=VMEM_LIMIT),
        cost_estimate=COST,
        name="attend",
    )(info, q, k, v, left, right, *before)


def backward_kernel(per, part, info, q_ref, k_ref, v_ref, left_ref, right_ref, mine_ref, theirs_ref, attn_ref, total_ref, *rest):
    dq_ref, own_ref, to_left_ref, to_right_ref, grad_ref = rest[-5:]
    step = pl.program_id(0)

    @pl.when(step == 0)
    def _():
        size = mine_ref.shape[0] // NZ
        for i in range(NZ):
            for ref, core in ((mine_ref, info[CORE_AT]), (theirs_ref, 1 - info[CORE_AT])):
                spot = pl.multiple_of((NC * i + core) * size, size)
                grad_ref[pl.ds(spot, size), :] = ref[i * size:(i + 1) * size, :]

    outs = (to_left_ref, own_ref, to_right_ref)
    live = live_sides(info)
    for i in range(per):
        cols = slice(i * HEAD, (i + 1) * HEAD)
        q = q_ref[:, cols]
        here = pl.multiple_of((step * per + i) * HEAD, HEAD)
        g = grad_ref[pl.ds(here, HEAD), :]
        total = total_ref[i]
        delta = jnp.sum(g.astype(F32) * attn_ref[cols, :].astype(F32), axis=0, keepdims=True)
        keys = (left_ref[0, :, cols], k_ref[:, cols], right_ref[0, :, cols])
        values = (left_ref[1, :, cols], v_ref[:, cols], right_ref[1, :, cols])
        dq = jnp.zeros((HEAD, q.shape[0]), F32)
        for j in range(3):
            k, v = keys[j], values[j]
            factor = LOG2_SCALE if j == 1 else jnp.where(live[j // 2], LOG2_SCALE, 0.0)
            shift = total if j == 1 else jnp.where(live[j // 2], total, FAR)
            w = jnp.exp2(nt(k, q) * factor - shift)
            outs[j][1, :, cols] = nt(w.astype(BF), g).astype(BF)
            ds = (w * (nn(v, g) - delta)).astype(BF)
            outs[j][0, :, cols] = (nn(ds, q) * SCALE).astype(BF)
            dq = dq + tn(k, ds)
        dq_ref[:, cols] = (dq * SCALE).T.astype(BF)


def attend_back(part, info, q, k, v, left, right, grads, attn, total, heads, before, again):
    rows, cols = q.shape
    per = PER_B
    own = pl.BlockSpec((rows, per * HEAD), lambda h, info: (0, info[part] // per + h))
    side = pl.BlockSpec((2, rows, per * HEAD), lambda h, info: (0, 0, h))
    turned = pl.BlockSpec((per * HEAD, rows), lambda h, info: (h, 0))
    return pl.pallas_call(
        functools.partial(backward_kernel, per, part),
        out_shape=(jax.ShapeDtypeStruct((rows, cols), BF),)
        + (jax.ShapeDtypeStruct((2, rows, heads * HEAD), BF),) * 3,
        grid_spec=pltpu.PrefetchScalarGridSpec(
            num_scalar_prefetch=1,
            grid=(heads // per,),
            in_specs=[own, own, own, side, side]
            + [pl.BlockSpec(grads[0].shape, lambda h, info: (0, 0))] * 2
            + [turned,
                      pl.BlockSpec((per, 1, rows), lambda h, info: (h, 0, 0))]
            + [pl.BlockSpec(memory_space=pl.ANY)] * len(before),
            out_specs=(own, side, side, side),
            scratch_shapes=[pltpu.VMEM((heads * HEAD, rows), BF)],
        ),
        input_output_aliases={10: 0} if again else {},
        compiler_params=pltpu.CompilerParams(vmem_limit_bytes=VMEM_LIMIT),
        cost_estimate=COST,
        name="attend_back",
    )(info, q, k, v, left, right, *grads, attn, total, *before)


JOIN_ROWS = 192


def join_kernel(first, info, own_ref, a_ref, b_ref, *rest):
    dk_ref, dv_ref = rest if first else rest[2:]
    for i, out in enumerate((dk_ref, dv_ref)):
        out[...] = (own_ref[i].astype(F32) + a_ref[i].astype(F32) + b_ref[i].astype(F32)).astype(BF)


def join(part, info, own, a, b, heads, cols, before):
    rows = own.shape[1]
    wide = heads * HEAD
    side = pl.BlockSpec((2, JOIN_ROWS, wide), lambda r, info: (0, r, 0))
    out = pl.BlockSpec((JOIN_ROWS, wide), lambda r, info: (r, info[part] // heads))
    first = before is None
    return pl.pallas_call(
        functools.partial(join_kernel, first),
        out_shape=(jax.ShapeDtypeStruct((rows, cols), BF),) * 2,
        grid_spec=pltpu.PrefetchScalarGridSpec(
            num_scalar_prefetch=1,
            grid=(rows // JOIN_ROWS,),
            in_specs=[side] * 3 + ([] if first else [pl.BlockSpec(memory_space=pl.ANY)] * 2),
            out_specs=(out, out),
        ),
        input_output_aliases={} if first else {4: 0, 5: 1},
        compiler_params=pltpu.CompilerParams(vmem_limit_bytes=VMEM_LIMIT),
        cost_estimate=COST,
        name="join",
    )(info, own, a, b, *(() if first else before))


def hold_kernel(x_ref, *rest):
    del x_ref, rest


def hold(x, *before):
    anywhere = pl.BlockSpec(memory_space=pl.ANY)
    return pl.pallas_call(
        hold_kernel,
        out_shape=jax.ShapeDtypeStruct(x.shape, x.dtype),
        in_specs=[anywhere] * (1 + len(before)),
        out_specs=anywhere,
        input_output_aliases={0: 0},
        cost_estimate=COST,
        name="hold",
    )(x, *before)


def window_kernel(part, info, k_ref, v_ref, *rest):
    out, sems = rest[-2:]
    wide = out.shape[2]
    cols = pl.ds(pl.multiple_of(info[part] * HEAD, wide), wide)
    copies = [
        pltpu.make_async_copy(ref.at[:, cols], out.at[j], sems.at[j])
        for j, ref in enumerate((k_ref, v_ref))
    ]
    for copy in copies:
        copy.start()
    for copy in copies:
        copy.wait()


def window(part, info, k, v, heads, before=()):
    rows = k.shape[0]
    return pl.pallas_call(
        functools.partial(window_kernel, part),
        out_shape=jax.ShapeDtypeStruct((2, rows, heads * HEAD), BF),
        in_specs=[pl.BlockSpec(memory_space=pltpu.SMEM)]
        + [pl.BlockSpec(memory_space=pl.ANY)] * (2 + len(before)),
        out_specs=pl.BlockSpec(memory_space=pltpu.VMEM),
        scratch_shapes=[pltpu.SemaphoreType.DMA((2,))],
        compiler_params=pltpu.CompilerParams(vmem_limit_bytes=VMEM_LIMIT),
        cost_estimate=COST,
        name="window",
    )(info, k, v, *before)


def project_back_kernel(place, *refs):
    pieces, (u_ref, other_ref) = refs[:NZ], refs[NZ:NZ + 2]
    mine_ref, theirs_ref, w = refs[-3:]
    rows = pieces[0].shape[0]
    for i, piece in enumerate(pieces):
        w[pl.ds(pl.multiple_of(place[FROM_Z + i] * rows, rows), rows), :] = piece[...]
    mine_ref[...] = nt(w[...], u_ref[...]).astype(BF)
    theirs_ref[...] = nt(w[...], other_ref[...]).astype(BF)


def project_back(place, pieces, u, other, before=()):
    rows, wide = pieces[0].shape
    tokens = u.shape[0]
    whole = pl.BlockSpec(memory_space=pltpu.VMEM)
    return pl.pallas_call(
        project_back_kernel,
        out_shape=(jax.ShapeDtypeStruct((NZ * rows, tokens), BF),) * 2,
        in_specs=[pl.BlockSpec(memory_space=pltpu.SMEM)] + [whole] * (NZ + 2)
        + [pl.BlockSpec(memory_space=pl.ANY)] * len(before),
        out_specs=(whole, whole),
        scratch_shapes=[pltpu.VMEM((NZ * rows, wide), BF)],
        compiler_params=pltpu.CompilerParams(vmem_limit_bytes=VMEM_LIMIT),
        cost_estimate=COST,
        name="project_back",
    )(place, *pieces, u, other, *before)


def project_kernel(place, *refs):
    turned, pieces = refs[:4], refs[4:4 + 2 * NZ]
    near_ref, far_refs, w = refs[-4], refs[-3:-1], refs[-1]
    rows = pieces[0].shape[0]
    half = NZ * rows
    for i, piece in enumerate(pieces):
        spot = (i // NZ) * half + place[FROM_Z + i % NZ] * rows
        w[pl.ds(pl.multiple_of(spot, rows), rows), :] = piece[...]
    wide = w.shape[1]
    block = wide // 4
    first, second = turned[2][...].T, turned[3][...].T
    for i in range(4):
        cols = slice(i * block, (i + 1) * block)
        there = slice(i % 2 * block, (i % 2 + 1) * block)
        total = nn(first, w[:half, cols]) + nn(second, w[half:, cols])
        far_refs[i // 2][:, there] = total.astype(BF)
    first, second = turned[0][...].T, turned[1][...].T
    for i in range(4):
        cols = slice(i * block, (i + 1) * block)
        near_ref[:, cols] = (nn(first, w[:half, cols]) + nn(second, w[half:, cols])).astype(BF)


def project(place, turned, pieces, before):
    tokens = turned[0].shape[1]
    rows, wide = pieces[0].shape
    whole = pl.BlockSpec(memory_space=pltpu.VMEM)
    return pl.pallas_call(
        project_kernel,
        out_shape=(jax.ShapeDtypeStruct((tokens, wide), BF),)
        + (jax.ShapeDtypeStruct((tokens, wide // 2), BF),) * 2,
        in_specs=[pl.BlockSpec(memory_space=pltpu.SMEM)] + [whole] * (4 + 2 * NZ)
        + [pl.BlockSpec(memory_space=pl.ANY)] * len(before),
        out_specs=(whole,) * 3,
        scratch_shapes=[pltpu.VMEM((2 * NZ * rows, wide), BF)],
        compiler_params=pltpu.CompilerParams(vmem_limit_bytes=VMEM_LIMIT),
        cost_estimate=COST,
        name="project",
    )(place, *turned, *pieces, *before)


def meet_kernel(near_ref, first_ref, second_ref, out_ref):
    half = first_ref.shape[1]
    for i, ref in enumerate((first_ref, second_ref)):
        cols = slice(i * half, (i + 1) * half)
        out_ref[:, cols] = (near_ref[:, cols].astype(F32) + ref[...].astype(F32)).astype(BF)


def meet(near, first, second):
    tokens, wide = near.shape
    block = 128
    spec = pl.BlockSpec((block, wide), lambda i: (i, 0))
    half = pl.BlockSpec((block, wide // 2), lambda i: (i, 0))
    return pl.pallas_call(
        meet_kernel,
        out_shape=jax.ShapeDtypeStruct((tokens, wide), BF),
        grid=(tokens // block,),
        in_specs=[spec, half, half],
        out_specs=spec,
        compiler_params=pltpu.CompilerParams(vmem_limit_bytes=VMEM_LIMIT),
        cost_estimate=COST,
        name="meet",
    )(near, first, second)


def weight_grad_kernel(place, *refs):
    a_refs, u_refs = refs[:4], refs[4:8]
    out_refs, total = refs[-1 - NZ:-1], refs[-1]
    left = jnp.concatenate([a[...] for a in a_refs], axis=1)
    right = jnp.concatenate([u[...] for u in u_refs], axis=0)
    total[...] = nn(left, right).astype(BF)
    rows = out_refs[0].shape[0]
    for i, out in enumerate(out_refs):
        out[...] = total[pl.ds(pl.multiple_of(place[TO_Z + i] * rows, rows), rows), :]


def weight_grad(place, a_list, u_list, before):
    rows, tokens = a_list[0].shape
    wide = u_list[0].shape[1]
    block = wide // WG_STEPS
    sub = rows // NZ
    return pl.pallas_call(
        weight_grad_kernel,
        out_shape=(jax.ShapeDtypeStruct((sub, wide), BF),) * NZ,
        grid_spec=pltpu.PrefetchScalarGridSpec(
            num_scalar_prefetch=1,
            grid=(WG_STEPS,),
            in_specs=[pl.BlockSpec((rows, tokens), lambda i, p: (0, 0))] * 4
            + [pl.BlockSpec((tokens, block), lambda i, p: (0, i))] * 4
            + [pl.BlockSpec(memory_space=pl.ANY)] * len(before),
            out_specs=(pl.BlockSpec((sub, block), lambda i, p: (0, i)),) * NZ,
            scratch_shapes=[pltpu.VMEM((rows, block), BF)],
        ),
        compiler_params=pltpu.CompilerParams(vmem_limit_bytes=VMEM_LIMIT),
        cost_estimate=COST,
        name="weight_grad",
    )(place, *a_list, *u_list, *before)


def sum_columns_kernel(place, *refs):
    pieces, outs = refs[:NZ], refs[-NY:]
    wide = outs[0].shape[1]
    for i, out in enumerate(outs):
        cols = pl.ds(pl.multiple_of(place[TO_Y + i] * wide, wide), wide)
        out[...] = sum(piece[:, cols].astype(F32) for piece in pieces).astype(out.dtype)


def sum_columns(place, pieces, before):
    rows, cols = pieces[0].shape
    whole = pl.BlockSpec(memory_space=pltpu.VMEM)
    return pl.pallas_call(
        sum_columns_kernel,
        out_shape=tuple(
            jax.ShapeDtypeStruct((rows, cols // NY), F32 if i == 0 else BF) for i in range(NY)
        ),
        in_specs=[pl.BlockSpec(memory_space=pltpu.SMEM)] + [whole] * NZ
        + [pl.BlockSpec(memory_space=pl.ANY)] * len(before),
        out_specs=(whole,) * NY,
        compiler_params=pltpu.CompilerParams(vmem_limit_bytes=VMEM_LIMIT),
        cost_estimate=COST,
        name="sum_columns",
    )(place, *pieces, *before)


def place_kernel(spots, *refs):
    out_ref = refs[-1]
    wide = refs[0].shape[1]
    for j, ref in enumerate(refs[:NY]):
        out_ref[:, pl.ds(pl.multiple_of(spots[FROM_Y + j] * wide, wide), wide)] = ref[...].astype(F32)


def place_columns(spots, pieces, before):
    rows, cols = pieces[0].shape
    whole = pl.BlockSpec(memory_space=pltpu.VMEM)
    return pl.pallas_call(
        place_kernel,
        out_shape=jax.ShapeDtypeStruct((rows, len(pieces) * cols), F32),
        in_specs=[pl.BlockSpec(memory_space=pltpu.SMEM)] + [whole] * NY
        + [pl.BlockSpec(memory_space=pl.ANY)] * len(before),
        out_specs=whole,
        cost_estimate=COST,
        name="place_columns",
    )(spots, *pieces, *before)


def add(*terms):
    return functools.reduce(lambda s, t: s + t.astype(F32), terms[1:], terms[0].astype(F32))


def on_device(query, key_in, value_in, out_weight, grad_out, neighbours):
    q, k, v, upstream = query[0], key_in[0], value_in[0], grad_out[0]
    rows, cols = q.shape
    half = cols // 2
    heads = half // HEAD
    dp = lax.axis_index("dp")
    tile = lax.axis_index("space")
    a, z, c = dp // (NZ * NC), (dp // NC) % NZ, dp % NC
    lo, y = tile // NY, tile % NY

    info = [a * heads, (1 - a) * heads, tile, c]
    info += [(z + i) % NZ for i in (0, 3, 1, 2)] + [(z + i) % NZ for i in range(NZ)]
    info += [(y + i) % NY for i in range(NY)] + [(y + i) % NY for i in (0, 3, 1, 2)]
    info = jnp.concatenate([jnp.stack(info).astype(jnp.int32), neighbours.reshape(-1)])
    pair = window(0, info, k, v, heads)
    near0 = (to_next(pair), to_previous(pair))
    up_core = move_core(upstream)

    def around(x):
        up, down = move_z(x, 1), move_z(x, 3)
        return [x, up, down]

    w0 = around(out_weight)
    w0[1] = hold(w0[1], up_core)
    later = window(1, info, k, v, heads, w0[1:2])
    pair = hold(later, *near0, *w0[1:])
    near1 = (to_next(pair), to_previous(pair))

    cross = move_cross(out_weight)
    w0.append(move_z(w0[1], 1))

    up_cross = move_cross(hold(upstream, cross))

    def back(w, before):
        mine, theirs = project_back(info, w, upstream, up_core, before)
        return mine, move_core(theirs)

    attn0, total0 = attend(0, info, q, k, v, *near0, heads)
    grad0 = back(w0, (attn0,))
    w1 = around(hold(cross, pair))
    dq, own0, to_left, to_right = attend_back(
        0, info, q, k, v, *near0, grad0, attn0, total0, heads, (w1[1], w1[2]), False
    )
    w1.append(move_z(hold(w1[0], grad0[0]), 2))
    attn1, total1 = attend(1, info, q, k, v, *near1, heads, (own0, w1[3]))
    up_cross = hold(up_cross, attn1)
    sent0 = (to_next(to_right), to_previous(to_left))

    def pick(attn, core):
        parts = attn.reshape(NZ, NC, -1, rows)
        sub = parts.shape[2]
        return lax.dynamic_slice(parts, (0, core, 0, 0), (NZ, 1, sub, rows)).reshape(
            NZ * sub, rows
        )

    own_part, core_part = pick(attn1, c), pick(attn1, 1 - c)
    a_list = [
        pick(attn0, c),
        move_core(pick(attn0, 1 - c)),
        move_cross(own_part),
        move_cross_core(core_part),
    ]
    grad1 = back(w1, (attn1,))
    core_far = move_core(core_part)
    dq, own1, to_left, to_right = attend_back(
        1, info, q, k, v, *near1, grad1, attn1, total1, heads, (dq, core_far), True
    )
    sent1 = (to_next(to_right), to_previous(to_left))
    u_list = [upstream, up_core, up_cross, move_core(up_cross)]
    pieces = weight_grad(info, a_list, u_list, (own1,))
    turned = [a_list[0], own_part, a_list[1], core_far]
    near, *far = project(info, turned, w0 + w1, pieces[:1] + sent0)
    mixed = meet(near, *[move_core(t) for t in far])
    done = join(0, info, own0, *sent0, heads, cols, None)
    done = join(1, info, own1, *sent1, heads, cols, done)

    columns = sum_columns(info, (pieces[0],) + tuple(move_z(pieces[i], i) for i in (1, 3, 2)), sent1)
    mine = add(columns[0], *[move_y(columns[i], i) for i in (1, 3, 2)]).astype(BF)
    mine = add(mine, move_lo(mine)).astype(BF)
    gathered = [mine] + [move_y(mine, i) for i in (1, 3, 2)]
    grad_weight = place_columns(info, gathered, (mixed,))
    dk, dv = done
    return (mixed[None], dq[None], dk[None], dv[None], grad_weight)


def solution(mesh):
    return jax.shard_map(
        on_device,
        mesh=mesh,
        in_specs=(
            P("dp", "space", None),
            P("dp", "space", None),
            P("dp", "space", None),
            P("dp", None),
            P("dp", "space", None),
            P(),
        ),
        out_specs=(
            P("dp", "space", None),
            P("dp", "space", None),
            P("dp", "space", None),
            P("dp", "space", None),
            P("dp", None),
        ),
        check_vma=False,
    )
```
